512 devices in a mesh: fsdp: 32 (over z_lo, x, core), replica: 16 (over z_hi, y).
Axes of the slice: x: 4, y: 4, z: 16 (z_hi: 4, z_lo: 4; z = z_hi * 4 + z_lo), core: 2. Of those that a mesh axis runs over, the one named last changes fastest.
Arguments:
- master: float32 [1792, 128, 128], P('fsdp', 'replica'), may hold values from -0.0625 to 0.0625
- gradient: bfloat16 [1792, 128, 128], P('fsdp', 'replica'), may hold values from -6 to 6
- first_moment: float32 [1792, 128, 128], P('fsdp', 'replica'), may hold values from -4 to 4
- second_moment: float32 [1792, 128, 128], P('fsdp', 'replica'), may hold values from 0.05 to 2
- owner_counts: int32 [32], replicated, may hold values from 1 to 84, 1792 in all
Outputs:
- master_new: float32 [1792, 128, 128], P('fsdp', 'replica')
- first_new: float32 [1792, 128, 128], P('fsdp', 'replica')
- second_new: float32 [1792, 128, 128], P('fsdp', 'replica')
- rollout_codes: bfloat16 [2688, 128, 128], P('fsdp')
- rollout_scales: bfloat16 [2688], P('fsdp')
The draws below stay inside these ranges and needn't reach their ends.
Inputs may be any that keep to these rules, and one draw needn't show every extreme that they name: owner_counts sum to 1792; the largest is exactly 84.
All inputs are finite; a program needn't handle non-finite values.
Results may differ from the reference program's by a relative error of at most 0.014.
Values may be sent and summed in bfloat16 or wider, within the bound.
A program may use at most 64 MiB of HBM per device.

```python
import math
import jax
import jax.numpy as jnp
import numpy as np
from jax import lax

D = 7168
BLOCK = 128
RB = 16
CB = 56
TILES = 1792
CAP_OWN = 84
N_FSDP = 32


def block_scale(own_key, dims, pieces, smallest, high):
    def one(dim, parts):
        steps = jax.random.uniform(jax.random.fold_in(jax.random.fold_in(own_key, 6), dim), (parts,), jnp.float32, smallest / len(pieces), high / len(pieces))
        return jnp.repeat(jnp.exp(steps), dims[dim] // parts).reshape((-1,) + (1,) * (len(dims) - dim - 1))

    gain = one(*pieces[0])
    for cut in pieces[1:]:
        gain = gain * one(*cut)
    return gain


def split_up(number_of, total, limit, skew):
    loads = [(1 << 20) // math.isqrt(grade ** skew) + 1 for grade in range(2, number_of + 1)]
    rest, counts = total - limit - (number_of - 1), [1] * (number_of - 1)
    while rest > 0:
        movable = [i for i in range(number_of - 1) if counts[i] < limit]
        mass, remaining = sum([loads[i] for i in movable]), rest
        for i in movable:
            addition = min(limit - counts[i], max(1, remaining * loads[i] // mass), rest)
            counts[i] = counts[i] + addition
            rest = rest - addition
    return np.array([limit] + counts)


def uneven(rng, count, total, reach, skew):
    if count == 2:
        one = jax.random.randint(rng, (), max(1, total - reach), min(reach, total - 1) + 1)
        return jnp.stack([one, total - one])
    sizes = jnp.asarray(split_up(count, total, reach, skew), jnp.int32)
    couples = (count - 1) // 2
    source_of, receiver = sizes[1:1 + 2 * couples:2], sizes[2:2 + 2 * couples:2]
    slack = jnp.minimum(source_of - 1, reach - receiver)
    shifted = jax.random.randint(jax.random.fold_in(rng, 1), (couples,), 0, 1 << 20) % (slack + 1)
    sizes = sizes.at[1:1 + 2 * couples:2].set(source_of - shifted).at[2:2 + 2 * couples:2].set(receiver + shifted)
    return sizes[jax.random.permutation(jax.random.fold_in(rng, 2), count)]


def bell_draw(key, extent, deviation, bound, shards=(), kind=jnp.bfloat16):
    values = jax.random.normal(key, extent, jnp.float32) * deviation
    if len(shards) > 0:
        values = block_scale(key, extent, shards, -0.22, 0.18) * values
    return jnp.clip(values, min=-bound, max=bound).astype(kind)


def setup_inputs(seed: int = 0) -> dict:
    key_of = jax.random.split(jax.random.key(seed), 6)
    master = bell_draw(key_of[0], (TILES, BLOCK, BLOCK), D ** -0.5, 0.0625, ((0, 32), (1, 16)), jnp.float32)
    gradient = bell_draw(key_of[1], (TILES, BLOCK, BLOCK), 1.0, 6.0, ((0, 32), (1, 16)))
    first_moment = bell_draw(key_of[2], (TILES, BLOCK, BLOCK), 0.3, 4.0, ((0, 32), (1, 16)), jnp.float32)
    second_moment = jnp.clip(jnp.exp(math.log(2.0) - 3.6888794 * jax.random.uniform(key_of[3], (TILES, BLOCK, BLOCK), jnp.float32) ** block_scale(key_of[3], (TILES, BLOCK, BLOCK), ((0, 32), (1, 16)), -0.2, 0.2)), 0.05, 2.0)
    owner_counts = uneven(key_of[4], N_FSDP, TILES, CAP_OWN, 2).astype(jnp.int32)
    return dict(master=master, gradient=gradient, first_moment=first_moment, second_moment=second_moment, owner_counts=owner_counts)


RATE = 0.003
BETA_ONE = 0.9
BETA_TWO = 0.95
EPSILON = 1e-08
DECAY = 0.1
CORRECT_ONE = 0.99997343861
CORRECT_TWO = 0.99407947

def learner_index_of(position):
    expert_of = position // (RB * CB)
    within = position % (RB * CB)
    col_block = within // RB
    row_block = within % RB
    return (expert_of * (RB * CB) + row_block * CB + col_block).astype(jnp.int32)

def reference(master, gradient, first_moment, second_moment, owner_counts):
    grad_float = gradient.astype(jnp.float32)
    first_new = BETA_ONE * first_moment + (1.0 - BETA_ONE) * grad_float
    second_new = BETA_TWO * second_moment + (1.0 - BETA_TWO) * grad_float * grad_float
    direction = first_new / CORRECT_ONE / (jnp.sqrt(second_new / CORRECT_TWO) + EPSILON)
    master_new = master - RATE * (direction + DECAY * master)
    block_peak = lax.optimization_barrier(jnp.max(jnp.abs(master_new), axis=(1, 2)))
    scales = (block_peak + 1e-06).astype(jnp.bfloat16)
    code_tiles = (master_new / scales.astype(jnp.float32)[:, None, None]).astype(jnp.bfloat16)
    range_end = jnp.cumsum(owner_counts).astype(jnp.int32)
    range_start = range_end - owner_counts
    position = jnp.arange(CAP_OWN, dtype=jnp.int32)
    filled = position[None, :] < owner_counts[:, None]
    wanted = jnp.where(filled, range_start[:, None] + position[None, :], 0).astype(jnp.int32).reshape(-1)
    source_ids = learner_index_of(wanted)
    filled_flat = filled.reshape(-1)
    zero_code = jnp.zeros((), jnp.bfloat16)
    rollout_codes = jnp.where(filled_flat[:, None, None], code_tiles[source_ids], zero_code)
    rollout_scales = jnp.where(filled_flat, scales[source_ids], zero_code)
    return (master_new, first_new, second_new, rollout_codes, rollout_scales)
```

```python
import functools

import jax
import jax.numpy as jnp
from jax import lax
from jax.experimental import pallas as pl
from jax.experimental.pallas import tpu as pltpu
from jax.sharding import PartitionSpec as P

MESH = pl.DeviceIdType.MESH

RB = 16
CB = 56
CAP_OWN = 84
HOLDERS = 32
COPIES = 16

RATE = 0.003
BETA_ONE = 0.9
BETA_TWO = 0.95
EPSILON = 1e-08
DECAY = 0.1
CORRECT_ONE = 0.99997343861
CORRECT_TWO = 0.99407947

ROWS = 8
LANES = 128
PER_PAIR = 6
OWN_ROWS = CAP_OWN * ROWS
PIECES = ((0, 256), (256, 256), (512, 160))
ALIKE = 32 * ROWS


def adam(master, gradient, first_moment, second_moment):
    grad_float = gradient.astype(jnp.float32)
    first_new = BETA_ONE * first_moment + (1.0 - BETA_ONE) * grad_float
    second_new = BETA_TWO * second_moment + (1.0 - BETA_TWO) * grad_float * grad_float
    direction = first_new / CORRECT_ONE / (jnp.sqrt(second_new / CORRECT_TWO) + EPSILON)
    master_new = master - RATE * (direction + DECAY * master)
    return master_new, first_new, second_new


def prepare(
    counts_ref, master_ref, gradient_ref, first_ref, second_ref,
    master_out, first_out, second_out, send, peak, place_ref,
    starts, raw,
):
    f = lax.axis_index("fsdp")
    e, r = f // RB, lax.rem(f, RB)

    pad = PER_PAIR * ROWS
    raw[pl.ds(0, pad), :] = jnp.zeros((pad, LANES), jnp.float32)
    raw[pl.ds(pad + CB * ROWS, pad), :] = jnp.zeros((pad, LANES), jnp.float32)
    lane = lax.broadcasted_iota(jnp.int32, (ROWS, LANES), 1)
    row = lax.broadcasted_iota(jnp.int32, (ROWS, LANES), 0)
    span = 8 * ROWS

    def update(step, peaks):
        here = pl.ds(pl.multiple_of(step * span, span), span)
        master_new, first_new, second_new = adam(
            master_ref[here, :], gradient_ref[here, :], first_ref[here, :], second_ref[here, :]
        )
        master_out[here, :] = master_new
        first_out[here, :] = first_new
        second_out[here, :] = second_new
        raw[pl.ds(pl.multiple_of(pad + step * span, 16), span), :] = master_new
        tall = jnp.max(jnp.abs(master_new).reshape(8, ROWS, LANES), axis=1)
        return jnp.where(lane == row + step * 8, jnp.max(tall, axis=1, keepdims=True), peaks)

    peaks = lax.fori_loop(0, CB // 8, update, jnp.zeros((ROWS, LANES), jnp.float32))
    peak[...] = jnp.broadcast_to(jnp.max(peaks, axis=0, keepdims=True), (ROWS, LANES))

    def total(o, start):
        starts[o] = start
        return start + counts_ref[o]

    lax.fori_loop(0, HOLDERS, total, 0)

    def pack(step, carry):
        first = ((starts[lax.rem(f + step, HOLDERS)] - r + (RB - 1)) >> 4) - CB * e
        first = jnp.clip(first, -PER_PAIR, CB) + PER_PAIR
        here = pl.ds(pl.multiple_of(first * ROWS, ROWS), PER_PAIR * ROWS)
        send[pl.ds(pl.multiple_of(step * 48, 16), 48), :] = raw[here, :].astype(jnp.bfloat16)
        return carry

    lax.fori_loop(0, HOLDERS, pack, 0)
    place_ref[pl.ds(0, 8), :] = jnp.full((ROWS, LANES), starts[f], jnp.int32)
    place_ref[pl.ds(8, 8), :] = jnp.full((ROWS, LANES), counts_ref[f], jnp.int32)


def exchange(
    send, first_peak, place_ref,
    all_ref, inverse_ref, scales_ref,
    recv, own, peak, peak_z, peak_y, table,
    a2a_send, a2a_recv, peak_send, peak_recv, gather_send, z_near, z_far, y_near, y_far, local_sem,
):
    f = lax.axis_index("fsdp")
    rep = lax.axis_index("replica")
    zh, y = rep // 4, lax.rem(rep, 4)

    def at_z(step):
        return {"replica": lax.rem(zh + step + 4, 4) * 4 + y}

    def at_y(step):
        return {"replica": zh * 4 + lax.rem(y + step + 4, 4)}

    def at_f(step):
        return {"fsdp": lax.rem(f + step, HOLDERS)}

    barrier = pltpu.get_barrier_semaphore()

    def greet(step, carry):
        pl.semaphore_signal(barrier, inc=1, device_id=at_f(step), device_id_type=MESH)
        return carry

    lax.fori_loop(1, HOLDERS, greet, 0)
    for step in (1, 2, 3):
        pl.semaphore_signal(barrier, inc=1, device_id=at_z(step), device_id_type=MESH)
        pl.semaphore_signal(barrier, inc=1, device_id=at_y(step), device_id_type=MESH)

    for piece in range(3):
        recv[pl.ds(piece * 512, 16), :] = send[pl.ds(piece * 16, 16), :]
    peak[...] = first_peak[...]
    lane = lax.broadcasted_iota(jnp.int32, (ROWS, LANES), 1)
    row = lax.broadcasted_iota(jnp.int32, (ROWS, LANES), 0)
    start = place_ref[pl.ds(0, 8), :]
    count = place_ref[pl.ds(8, 8), :]
    odd = [(start & (1 << bit)) != 0 for bit in range(4)]

    pl.semaphore_wait(barrier, HOLDERS - 1 + 6)

    for piece in range(3):

        def give(step, carry, piece=piece):
            pltpu.make_async_remote_copy(
                src_ref=send.at[pl.ds(pl.multiple_of(step * 48 + piece * 16, 16), 16)],
                dst_ref=recv.at[pl.ds(pl.multiple_of(piece * 512 + step * 16, 16), 16)],
                send_sem=a2a_send,
                recv_sem=a2a_recv.at[piece],
                device_id=at_f(step),
                device_id_type=MESH,
            ).start()
            return carry

        lax.fori_loop(1, HOLDERS, give, 0)

    def tell(source, target, send_sem, recv_sem, device):
        copy = pltpu.make_async_remote_copy(
            src_ref=source, dst_ref=target, send_sem=send_sem, recv_sem=recv_sem, device_id=device, device_id_type=MESH
        )
        copy.start()

    def landed(target, sem):
        pltpu.make_async_copy(target, target, sem).wait()

    for step in (1, 2, 3):
        tell(peak, peak_z.at[pl.ds((step - 1) * 8, 8)], peak_send.at[0], peak_recv.at[0], at_z(step))

    def order(piece):
        halves = [[], []]
        for r in range(RB):
            found = []
            for e in range(2):
                away = lax.rem(f - (e * RB + r) + HOLDERS, HOLDERS)
                pair = recv[pl.ds(pl.multiple_of(piece * 512 + away * 16, 16), 16), :]
                found.append(pair.astype(jnp.float32))
            position = start + ((r - start) & (RB - 1)) + piece * 32
            for half in range(2):
                here = slice(half * 8, half * 8 + 8)
                late = position >= RB * CB - half * 16
                halves[half].append(jnp.where(late, found[1][here, :], found[0][here, :]))
        for half in range(2):
            tiles = halves[half]
            for bit in range(4):
                tiles = [jnp.where(odd[bit], tiles[(k + (1 << bit)) % RB], tiles[k]) for k in range(RB)]
            slots = min(RB, PIECES[piece][1] // ROWS - half * RB)
            for k in range(0, slots, 2):
                both = jnp.concatenate([tiles[k], tiles[k + 1]], axis=0).astype(jnp.bfloat16)
                own[pl.ds((piece * 32 + half * 16 + k) * ROWS, 16), :] = both

    def chunk(z, yy, low, number):
        place = (z * 4 + yy) * OWN_ROWS + low
        return all_ref.at[pl.ds(pl.multiple_of(place, 16), number)]

    def z_at(step):
        return lax.rem(zh + step + 4, 4)

    def y_at(step):
        return lax.rem(y + step + 4, 4)

    def send_y(z_step, piece):
        low, number = PIECES[piece]
        place = chunk(z_at(z_step), y, low, number)
        source = own.at[pl.ds(low, number)] if z_step == 0 else place
        for way, step in enumerate((1, -1)):
            tell(source, place, gather_send, y_near.at[way, z_step, piece], at_y(step))

    locals_ = []
    for piece, (low, number) in enumerate(PIECES):
        landed(recv.at[pl.ds(piece * 512 + 16, 31 * 16)], a2a_recv.at[piece])
        order(piece)
        here = own.at[pl.ds(low, number)]
        for way, step in enumerate((1, -1)):
            tell(here, chunk(zh, y, low, number), gather_send, z_near.at[way, piece], at_z(step))
        send_y(0, piece)
        keep = pltpu.make_async_copy(here, chunk(zh, y, low, number), local_sem.at[piece])
        keep.start()
        locals_.append(keep)

    def relay_z(piece):
        low, number = PIECES[piece]
        part = number // 2
        for way, step in enumerate((1, -1)):
            landed(chunk(z_at(-step), y, low, number), z_near.at[way, piece])
            half = chunk(z_at(-step), y, low + way * part, part)
            tell(half, half, gather_send, z_far.at[way, piece], at_z(step))
            send_y((-step) % 4, piece)

    def finish_z(piece):
        low, number = PIECES[piece]
        part = number // 2
        for way in range(2):
            landed(chunk(z_at(2), y, low + way * part, part), z_far.at[way, piece])
        send_y(2, piece)

    def relay_y(z_step, piece):
        low, number = PIECES[piece]
        part = number // 2
        for way, step in enumerate((1, -1)):
            landed(chunk(z_at(z_step), y_at(-step), low, number), y_near.at[way, z_step, piece])
            half = chunk(z_at(z_step), y_at(-step), low + way * part, part)
            tell(half, half, gather_send, y_far.at[way, z_step, piece], at_y(step))

    def peaks_y():
        landed(peak_z, peak_recv.at[0])
        landed(peak_z, peak_send.at[0])
        best = peak[...]
        for step in range(3):
            best = jnp.maximum(best, peak_z[pl.ds(step * 8, 8), :])
        peak[...] = best
        for step in (1, 2, 3):
            tell(peak, peak_y.at[pl.ds((step - 1) * 8, 8)], peak_send.at[1], peak_recv.at[1], at_y(step))

    def peaks_f():
        landed(peak_y, peak_recv.at[1])
        landed(peak_y, peak_send.at[1])
        best = peak[...]
        for step in range(3):
            best = jnp.maximum(best, peak_y[pl.ds(step * 8, 8), :])
        table[pl.ds(0, 8), :] = best

        def spread(step, carry):
            tell(
                table.at[pl.ds(0, 8)],
                table.at[pl.ds(pl.multiple_of(step * 8, 8), 8)],
                peak_send.at[2],
                peak_recv.at[2],
                at_f(step),
            )
            return carry

        lax.fori_loop(1, HOLDERS, spread, 0)

    def scales():
        others = table.at[pl.ds(8, 31 * 8)]
        landed(others, peak_recv.at[2])
        landed(others, peak_send.at[2])

        flat = jnp.zeros((ROWS, LANES), jnp.float32)
        for step in range(11):
            slot = step * 8 + row
            u = start + slot
            late = u >= RB * CB
            away = (f - (u & (RB - 1)) - jnp.where(late, RB, 0)) & (HOLDERS - 1)
            found = jnp.zeros((ROWS, LANES), jnp.float32)
            for source in range(HOLDERS):
                found = jnp.where(away == source, table[pl.ds(source * 8, 8), :], found)
            column = (u >> 4) - jnp.where(late, CB, 0)
            top = jnp.max(jnp.where(lane == column, found, 0.0), axis=1, keepdims=True)
            scale = jnp.broadcast_to((top + 1e-06).astype(jnp.bfloat16).astype(jnp.float32), (ROWS, LANES))
            filled = slot < count
            inverse_ref[pl.ds(step * 8, 8), :] = jnp.where(filled, 1.0 / scale, 0.0)
            flat = jnp.where((lane == slot) & filled, scale, flat)
        scales_ref[...] = jnp.broadcast_to(jnp.max(flat, axis=0, keepdims=True), (ROWS, LANES))

    relay_y(0, 0)
    relay_z(0)
    peaks_y()
    relay_y(0, 1)
    relay_z(1)
    relay_y(0, 2)
    peaks_f()
    relay_y(1, 0)
    relay_y(3, 0)
    finish_z(0)
    relay_z(2)
    relay_y(1, 1)
    relay_y(3, 1)
    finish_z(1)
    scales()
    relay_y(2, 0)
    finish_z(2)
    relay_y(1, 2)
    relay_y(3, 2)
    relay_y(2, 1)
    relay_y(2, 2)
    for piece, (low, number) in enumerate(PIECES):
        part = number // 2
        for z_step in range(4):
            for way in range(2):
                landed(chunk(z_at(z_step), y_at(2), low + way * part, part), y_far.at[way, z_step, piece])
    for keep in locals_:
        keep.wait()
    landed(send.at[pl.ds(48, 31 * 48)], a2a_send)
    landed(all_ref.at[pl.ds(0, 15 * OWN_ROWS)], gather_send)


def finish(all_ref, inverse_ref, codes_ref):
    inverse = inverse_ref[...][:, None, :]
    for pair in range(COPIES // 2):
        parts = [all_ref[2 * pair + i].astype(jnp.float32).reshape(8, ROWS, LANES) for i in range(2)]
        both = jnp.concatenate(parts, axis=1)
        codes = jnp.where(inverse > 0.0, both * inverse, 0.0)
        codes_ref[:, pl.ds(pair * 16, 16), :] = codes.astype(jnp.bfloat16)


def on_device(master, gradient, first_moment, second_moment, owner_counts):
    tiles, rows, lanes = master.shape
    flat = [a.reshape(tiles * rows, lanes) for a in (master, gradient, first_moment, second_moment)]
    vmem = pl.BlockSpec(memory_space=pltpu.VMEM)
    dma = pltpu.SemaphoreType.DMA
    part = jax.ShapeDtypeStruct((tiles * rows, lanes), jnp.float32)
    tile = jax.ShapeDtypeStruct((ROWS, LANES), jnp.float32)
    master_new, first_new, second_new, send, peak, place = pl.pallas_call(
        prepare,
        out_shape=(
            part, part, part,
            jax.ShapeDtypeStruct((HOLDERS * 48, LANES), jnp.bfloat16),
            tile,
            jax.ShapeDtypeStruct((2 * ROWS, LANES), jnp.int32),
        ),
        in_specs=[pl.BlockSpec(memory_space=pltpu.SMEM)] + [vmem] * 4,
        out_specs=(vmem,) * 6,
        scratch_shapes=[
            pltpu.SMEM((HOLDERS,), jnp.int32),
            pltpu.VMEM(((CB + 2 * PER_PAIR) * ROWS, LANES), jnp.float32),
        ],
        name="prepare",
    )(owner_counts, *flat)
    gathered, inverse, scales = pl.pallas_call(
        exchange,
        out_shape=(
            jax.ShapeDtypeStruct((COPIES * OWN_ROWS, LANES), jnp.bfloat16),
            jax.ShapeDtypeStruct((88, LANES), jnp.float32),
            tile,
        ),
        in_specs=[vmem] * 3,
        out_specs=(vmem, vmem, vmem),
        scratch_shapes=[
            pltpu.VMEM((3 * 512, LANES), jnp.bfloat16),
            pltpu.VMEM((OWN_ROWS, LANES), jnp.bfloat16),
            pltpu.VMEM((ROWS, LANES), jnp.float32),
            pltpu.VMEM((3 * ROWS, LANES), jnp.float32),
            pltpu.VMEM((3 * ROWS, LANES), jnp.float32),
            pltpu.VMEM((HOLDERS * ROWS, LANES), jnp.float32),
            dma,
            dma((3,)),
            dma((3,)),
            dma((3,)),
            dma,
            dma((2, 3)),
            dma((2, 3)),
            dma((2, 4, 3)),
            dma((2, 4, 3)),
            dma((3,)),
        ],
        compiler_params=pltpu.CompilerParams(collective_id=0, has_side_effects=True, vmem_limit_bytes=40 << 20),
        name="exchange",
    )(send, peak, place)
    codes = pl.pallas_call(
        finish,
        grid=(11,),
        out_shape=jax.ShapeDtypeStruct((CAP_OWN, 128, 128), jnp.bfloat16),
        in_specs=[
            pl.BlockSpec((COPIES, 8 * ROWS, LANES), lambda i: (0, i, 0)),
            pl.BlockSpec((8, LANES), lambda i: (i, 0)),
        ],
        out_specs=pl.BlockSpec((8, 128, 128), lambda i: (i, 0, 0)),
        compiler_params=pltpu.CompilerParams(vmem_limit_bytes=40 << 20),
        name="finish",
    )(gathered.reshape(COPIES, OWN_ROWS, LANES), inverse)
    shape = (tiles, rows, lanes)
    rollout_scales = scales[0, :CAP_OWN].astype(jnp.bfloat16)
    return master_new.reshape(shape), first_new.reshape(shape), second_new.reshape(shape), codes, rollout_scales


def solution(mesh):
    split = P("fsdp", "replica", None)
    return jax.shard_map(
        on_device,
        mesh=mesh,
        in_specs=(split, split, split, split, P()),
        out_specs=(split, split, split, P("fsdp", None, None), P("fsdp")),
        check_vma=False,
    )
```

```python
import functools

import jax
import jax.numpy as jnp
from jax import lax
from jax.experimental import pallas as pl
from jax.experimental.pallas import tpu as pltpu
from jax.sharding import PartitionSpec as P

MESH = pl.DeviceIdType.MESH

RB = 16
CB = 56
CAP_OWN = 84
HOLDERS = 32
COPIES = 16

RATE = 0.003
BETA_ONE = 0.9
BETA_TWO = 0.95
EPSILON = 1e-08
DECAY = 0.1
CORRECT_ONE = 0.99997343861
CORRECT_TWO = 0.99407947

ROWS = 8
LANES = 128
PER_PAIR = 6
OWN_ROWS = CAP_OWN * ROWS
PIECES = ((0, 256), (256, 256), (512, 160))
VMEM_LIMIT = 63 << 20
GROUP = 16
REACH = 22


def adam(master, gradient, first_moment, second_moment):
    grad_float = gradient.astype(jnp.float32)
    first_new = BETA_ONE * first_moment + (1.0 - BETA_ONE) * grad_float
    second_new = BETA_TWO * second_moment + (1.0 - BETA_TWO) * grad_float * grad_float
    direction = first_new / CORRECT_ONE / (jnp.sqrt(second_new / CORRECT_TWO) + EPSILON)
    master_new = master - RATE * (direction + DECAY * master)
    return master_new, first_new, second_new


def exchange(
    counts_ref, master_in, gradient_in, first_in, second_in,
    all_ref, inverse_ref, scales_ref,
    master_ref, gradient_ref, first_ref, second_ref, in_sem, raw, send, recv, own, peak, peak_z, peak_y, table,
    a2a_send, a2a_recv, peak_send, peak_recv, gather_send, z_near, z_far, y_near, y_far, local_sem,
):
    f = lax.axis_index("fsdp")
    rep = lax.axis_index("replica")
    zh, y = rep // 4, lax.rem(rep, 4)
    e, r = f // RB, lax.rem(f, RB)
    lowest = e * (HOLDERS - REACH)
    wide = (f >= HOLDERS - REACH) & (f < REACH)

    def at_z(step):
        return {"replica": lax.rem(zh + step + 4, 4) * 4 + y}

    def at_y(step):
        return {"replica": zh * 4 + lax.rem(y + step + 4, 4)}

    def at_f(step):
        return {"fsdp": lax.rem(f + step, HOLDERS)}

    inputs = ((master_in, master_ref), (gradient_in, gradient_ref), (first_in, first_ref), (second_in, second_ref))
    inputs = [pltpu.make_async_copy(source, target, in_sem.at[i]) for i, (source, target) in enumerate(inputs)]
    for copy in inputs:
        copy.start()
    barrier = pltpu.get_barrier_semaphore()

    def greet(step, carry):
        source = lax.rem(f + step, HOLDERS)

        @pl.when(((source < RB) & (f < REACH)) | ((source >= RB) & (f >= HOLDERS - REACH)))
        def _():
            pl.semaphore_signal(barrier, inc=1, device_id={"fsdp": source}, device_id_type=MESH)

        return carry

    lax.fori_loop(1, HOLDERS, greet, 0)
    for step in (1, 2, 3):
        pl.semaphore_signal(barrier, inc=1, device_id=at_z(step), device_id_type=MESH)
        pl.semaphore_signal(barrier, inc=1, device_id=at_y(step), device_id_type=MESH)

    lane = lax.broadcasted_iota(jnp.int32, (ROWS, LANES), 1)
    row = lax.broadcasted_iota(jnp.int32, (ROWS, LANES), 0)
    for copy in inputs:
        copy.wait()
    span = 8 * ROWS
    peaks = jnp.zeros((ROWS, LANES), jnp.float32)
    for step in range(CB // 8):
        here = pl.ds(step * span, span)
        master_new, _, _ = adam(master_ref[here, :], gradient_ref[here, :], first_ref[here, :], second_ref[here, :])
        raw[here, :] = master_new.astype(jnp.bfloat16)
        tall = jnp.max(jnp.abs(master_new).reshape(8, ROWS, LANES), axis=1)
        peaks = jnp.where(lane == row + step * 8, jnp.max(tall, axis=1, keepdims=True), peaks)
    peak[...] = jnp.broadcast_to(jnp.max(peaks, axis=0, keepdims=True), (ROWS, LANES))

    begins = [jnp.int32(0)]
    for o in range(HOLDERS - 1):
        begins.append(begins[-1] + counts_ref[o])
    line = lax.broadcasted_iota(jnp.int32, (48, LANES), 0)
    column = lax.broadcasted_iota(jnp.int32, (48, LANES), 1)
    for i in range(REACH):
        begin = begins[i] + e * (begins[i + HOLDERS - REACH] - begins[i])
        first = ((jnp.full((48, LANES), begin, jnp.int32) - r + (RB - 1)) >> 4) - CB * e
        place = first * ROWS + line - column
        packed = jnp.zeros((48, LANES), jnp.float32)
        for low in range(0, CB * ROWS, LANES):
            width = min(LANES, CB * ROWS - low)
            ones = jnp.where(place == low, 1.0, 0.0).astype(jnp.bfloat16)[:, :width]
            packed += jnp.dot(ones, raw[pl.ds(low, width), :], preferred_element_type=jnp.float32)
        send[pl.ds(i * 48, 48), :] = packed.astype(jnp.bfloat16)
    for piece in range(3):
        mine = send[pl.ds(pl.multiple_of((f - lowest) * 48 + piece * 16, 16), 16), :]
        recv[pl.ds(pl.multiple_of(piece * 512 + f * 16, 16), 16), :] = mine

    begin = begins[HOLDERS - 1] * 0
    for o in range(1, HOLDERS):
        begin += jnp.where(f == o, 1, 0) * begins[o]
    start = jnp.full((ROWS, LANES), begin, jnp.int32)
    count = jnp.full((ROWS, LANES), counts_ref[f], jnp.int32)
    odd = [(start & (1 << bit)) != 0 for bit in range(4)]

    pl.semaphore_wait(barrier, REACH - 1 + 6)

    def owners(give):
        def visit(step, carry):
            i = lax.rem(f + step, REACH)

            @pl.when(lowest + i != f)
            def _():
                give(i)

            return carry

        lax.fori_loop(0, REACH, visit, 0)

    for piece in range(3):

        def give(i, piece=piece):
            pltpu.make_async_remote_copy(
                src_ref=send.at[pl.ds(pl.multiple_of(i * 48 + piece * 16, 16), 16)],
                dst_ref=recv.at[pl.ds(pl.multiple_of(piece * 512 + f * 16, 16), 16)],
                send_sem=a2a_send,
                recv_sem=a2a_recv.at[piece],
                device_id={"fsdp": lowest + i},
                device_id_type=MESH,
            ).start()

        owners(give)

    def tell(source, target, send_sem, recv_sem, device):
        copy = pltpu.make_async_remote_copy(
            src_ref=source, dst_ref=target, send_sem=send_sem, recv_sem=recv_sem, device_id=device, device_id_type=MESH
        )
        copy.start()

    def landed(target, sem):
        pltpu.make_async_copy(target, target, sem).wait()

    def landed_from_all(buffer, low, rows, sem):
        @pl.when(wide)
        def _():
            landed(buffer.at[pl.ds(low, (HOLDERS - 1) * rows)], sem)

        @pl.when(jnp.logical_not(wide))
        def _():
            landed(buffer.at[pl.ds(low, (RB - 1) * rows)], sem)

    for step in (1, 2, 3):
        tell(peak, peak_z.at[pl.ds((step - 1) * 8, 8)], peak_send.at[0], peak_recv.at[0], at_z(step))

    def order(piece):
        halves = [[], []]
        for r in range(RB):
            found = []
            for e in range(2):
                pair = recv[pl.ds(piece * 512 + (e * RB + r) * 16, 16), :]
                found.append(pair.astype(jnp.float32))
            position = start + ((r - start) & (RB - 1)) + piece * 32
            for half in range(2):
                here = slice(half * 8, half * 8 + 8)
                late = position >= RB * CB - half * 16
                halves[half].append(jnp.where(late, found[1][here, :], found[0][here, :]))
        for half in range(2):
            tiles = halves[half]
            for bit in range(4):
                tiles = [jnp.where(odd[bit], tiles[(k + (1 << bit)) % RB], tiles[k]) for k in range(RB)]
            slots = min(RB, PIECES[piece][1] // ROWS - half * RB)
            for k in range(0, slots, 2):
                both = jnp.concatenate([tiles[k], tiles[k + 1]], axis=0).astype(jnp.bfloat16)
                own[pl.ds((piece * 32 + half * 16 + k) * ROWS, 16), :] = both

    def chunk(z, yy, low, number):
        place = (z * 4 + yy) * OWN_ROWS + low
        return all_ref.at[pl.ds(pl.multiple_of(place, 16), number)]

    def z_at(step):
        return lax.rem(zh + step + 4, 4)

    def y_at(step):
        return lax.rem(y + step + 4, 4)

    def send_y(z_step, piece):
        low, number = PIECES[piece]
        place = chunk(z_at(z_step), y, low, number)
        source = own.at[pl.ds(low, number)] if z_step == 0 else place
        for way, step in enumerate((1, -1)):
            tell(source, place, gather_send, y_near.at[way, z_step, piece], at_y(step))

    locals_ = []
    for piece, (low, number) in enumerate(PIECES):
        landed_from_all(recv, piece * 512, 16, a2a_recv.at[piece])
        order(piece)
        here = own.at[pl.ds(low, number)]
        for way, step in enumerate((1, -1)):
            tell(here, chunk(zh, y, low, number), gather_send, z_near.at[way, piece], at_z(step))
        send_y(0, piece)
        keep = pltpu.make_async_copy(here, chunk(zh, y, low, number), local_sem.at[piece])
        keep.start()
        locals_.append(keep)

    def relay_z(piece):
        low, number = PIECES[piece]
        part = number // 2
        for way, step in enumerate((1, -1)):
            landed(chunk(z_at(-step), y, low, number), z_near.at[way, piece])
            half = chunk(z_at(-step), y, low + way * part, part)
            tell(half, half, gather_send, z_far.at[way, piece], at_z(step))
            send_y((-step) % 4, piece)

    def finish_z(piece):
        low, number = PIECES[piece]
        part = number // 2
        for way in range(2):
            landed(chunk(z_at(2), y, low + way * part, part), z_far.at[way, piece])
        send_y(2, piece)

    def relay_y(z_step, piece):
        low, number = PIECES[piece]
        part = number // 2
        for way, step in enumerate((1, -1)):
            landed(chunk(z_at(z_step), y_at(-step), low, number), y_near.at[way, z_step, piece])
            half = chunk(z_at(z_step), y_at(-step), low + way * part, part)
            tell(half, half, gather_send, y_far.at[way, z_step, piece], at_y(step))

    def peaks_y():
        landed(peak_z, peak_recv.at[0])
        landed(peak_z, peak_send.at[0])
        best = peak[...]
        for step in range(3):
            best = jnp.maximum(best, peak_z[pl.ds(step * 8, 8), :])
        peak[...] = best
        for step in (1, 2, 3):
            tell(peak, peak_y.at[pl.ds((step - 1) * 8, 8)], peak_send.at[1], peak_recv.at[1], at_y(step))

    def peaks_f():
        landed(peak_y, peak_recv.at[1])
        landed(peak_y, peak_send.at[1])
        best = peak[...]
        for step in range(3):
            best = jnp.maximum(best, peak_y[pl.ds(step * 8, 8), :])
        mine = table.at[pl.ds(pl.multiple_of(f * 8, 8), 8)]
        mine[...] = best

        def give(i):
            tell(mine, mine, peak_send.at[2], peak_recv.at[2], {"fsdp": lowest + i})

        owners(give)

    def scales():
        landed_from_all(table, 0, 8, peak_recv.at[2])
        landed(table.at[pl.ds(0, (REACH - 1) * 8)], peak_send.at[2])

        flat = jnp.zeros((ROWS, LANES), jnp.float32)
        for step in range(11):
            slot = step * 8 + row
            u = start + slot
            late = u >= RB * CB
            origin = (u & (RB - 1)) + jnp.where(late, RB, 0)
            found = jnp.zeros((ROWS, LANES), jnp.float32)
            for source in range(HOLDERS):
                found = jnp.where(origin == source, table[pl.ds(source * 8, 8), :], found)
            column = (u >> 4) - jnp.where(late, CB, 0)
            top = jnp.max(jnp.where(lane == column, found, 0.0), axis=1, keepdims=True)
            scale = jnp.broadcast_to((top + 1e-06).astype(jnp.bfloat16).astype(jnp.float32), (ROWS, LANES))
            filled = slot < count
            inverse_ref[pl.ds(step * 8, 8), :] = jnp.where(filled, 1.0 / scale, 0.0)
            flat = jnp.where((lane == slot) & filled, scale, flat)
        scales_ref[...] = jnp.broadcast_to(jnp.max(flat, axis=0, keepdims=True), (ROWS, LANES))

    relay_y(0, 0)
    relay_z(0)
    peaks_y()
    relay_y(0, 1)
    relay_z(1)
    relay_y(0, 2)
    peaks_f()
    relay_y(1, 0)
    relay_y(3, 0)
    finish_z(0)
    relay_z(2)
    relay_y(1, 1)
    relay_y(3, 1)
    finish_z(1)
    scales()
    relay_y(2, 0)
    finish_z(2)
    relay_y(1, 2)
    relay_y(3, 2)
    relay_y(2, 1)
    relay_y(2, 2)
    for piece, (low, number) in enumerate(PIECES):
        part = number // 2
        for z_step in range(4):
            for way in range(2):
                landed(chunk(z_at(z_step), y_at(2), low + way * part, part), y_far.at[way, z_step, piece])
    for keep in locals_:
        keep.wait()
    landed(send.at[pl.ds(0, (REACH - 1) * 48)], a2a_send)
    landed(all_ref.at[pl.ds(0, 15 * OWN_ROWS)], gather_send)


def finish(
    all_ref, inverse_ref, scale_ref, master_ref, gradient_ref, first_ref, second_ref,
    codes_ref, scales_ref, master_out, first_out, second_out,
    tiles, codes, inverse, master, gradient, first, second, master_to, first_to, second_to,
    tile_sem, small_sem, out_sem,
):
    def started(source, target, sem):
        copy = pltpu.make_async_copy(source, target, sem)
        copy.start()
        return copy

    small = [
        started(source, target, small_sem.at[i])
        for i, (source, target) in enumerate(
            ((master_ref, master), (gradient_ref, gradient), (first_ref, first), (second_ref, second), (inverse_ref, inverse))
        )
    ]
    steps = [(low, min(GROUP, CAP_OWN - low)) for low in range(0, CAP_OWN, GROUP)]
    arriving = []
    for i, (low, slots) in enumerate(steps):
        rows = pl.ds(low * ROWS, slots * ROWS)
        arriving.append(started(all_ref.at[:, rows, :], tiles.at[:, rows, :], tile_sem.at[i]))
    for copy in small:
        copy.wait()
    leaving = []
    span = 8 * ROWS

    def update(step, carry):
        here = pl.ds(pl.multiple_of(step * span, span), span)
        master_new, first_new, second_new = adam(master[here, :], gradient[here, :], first[here, :], second[here, :])
        master_to[here, :] = master_new
        first_to[here, :] = first_new
        second_to[here, :] = second_new
        return carry

    lax.fori_loop(0, CB // 8, update, 0)
    for i, (source, target) in enumerate(((master_to, master_out), (first_to, first_out), (second_to, second_out))):
        leaving.append(started(source, target, out_sem.at[i]))
    for i, (low, slots) in enumerate(steps):
        arriving[i].wait()
        for base in range(low, low + slots, 8):
            number = min(8, CAP_OWN - base)
            factor = inverse[pl.ds(base, number), :][:, None, :]
            for pair in range(COPIES // 2):
                parts = [
                    tiles[2 * pair + k, pl.ds(base * ROWS, number * ROWS), :].astype(jnp.float32).reshape(number, ROWS, LANES)
                    for k in range(2)
                ]
                both = jnp.concatenate(parts, axis=1)
                coded = jnp.where(factor > 0.0, both * factor, 0.0).astype(jnp.bfloat16)
                codes[pl.ds(base, number), pl.ds(pair * 16, 16), :] = coded
        here = pl.ds(low, slots)
        leaving.append(started(codes.at[here], codes_ref.at[here], out_sem.at[3 + i]))
    scales_ref[...] = scale_ref[0, :][:CAP_OWN].astype(jnp.bfloat16)
    for copy in leaving:
        copy.wait()


def on_device(master, gradient, first_moment, second_moment, owner_counts):
    tiles, rows, lanes = master.shape
    flat = [a.reshape(tiles * rows, lanes) for a in (master, gradient, first_moment, second_moment)]
    vmem = pl.BlockSpec(memory_space=pltpu.VMEM)
    hbm = pl.BlockSpec(memory_space=pl.ANY)
    dma = pltpu.SemaphoreType.DMA
    part = jax.ShapeDtypeStruct((tiles * rows, lanes), jnp.float32)
    tile = jax.ShapeDtypeStruct((ROWS, LANES), jnp.float32)
    own = pltpu.VMEM((tiles * rows, lanes), jnp.float32)
    gathered, inverse, scales = pl.pallas_call(
        exchange,
        out_shape=(
            jax.ShapeDtypeStruct((COPIES * OWN_ROWS, LANES), jnp.bfloat16),
            jax.ShapeDtypeStruct((88, LANES), jnp.float32),
            tile,
        ),
        in_specs=[pl.BlockSpec(memory_space=pltpu.SMEM)] + [hbm] * 4,
        out_specs=(vmem, vmem, vmem),
        scratch_shapes=[
            own, pltpu.VMEM((tiles * rows, lanes), jnp.bfloat16), own, own,
            dma((4,)),
            pltpu.VMEM((CB * ROWS, LANES), jnp.bfloat16),
            pltpu.VMEM((REACH * 48, LANES), jnp.bfloat16),
            pltpu.VMEM((3 * 512, LANES), jnp.bfloat16),
            pltpu.VMEM((OWN_ROWS, LANES), jnp.bfloat16),
            pltpu.VMEM((ROWS, LANES), jnp.float32),
            pltpu.VMEM((3 * ROWS, LANES), jnp.float32),
            pltpu.VMEM((3 * ROWS, LANES), jnp.float32),
            pltpu.VMEM((HOLDERS * ROWS, LANES), jnp.float32),
            dma,
            dma((3,)),
            dma((3,)),
            dma((3,)),
            dma,
            dma((2, 3)),
            dma((2, 3)),
            dma((2, 4, 3)),
            dma((2, 4, 3)),
            dma((3,)),
        ],
        compiler_params=pltpu.CompilerParams(collective_id=0, has_side_effects=True, vmem_limit_bytes=VMEM_LIMIT),
        name="exchange",
    )(owner_counts, *flat)
    steps = -(-CAP_OWN // GROUP)
    codes, rollout_scales, master_new, first_new, second_new = pl.pallas_call(
        finish,
        out_shape=(
            jax.ShapeDtypeStruct((CAP_OWN, 128, 128), jnp.bfloat16),
            jax.ShapeDtypeStruct((CAP_OWN,), jnp.bfloat16),
            part, part, part,
        ),
        in_specs=[hbm, hbm, vmem] + [hbm] * 4,
        out_specs=(hbm, vmem, hbm, hbm, hbm),
        scratch_shapes=[
            pltpu.VMEM((COPIES, OWN_ROWS, LANES), jnp.bfloat16),
            pltpu.VMEM((CAP_OWN, 128, 128), jnp.bfloat16),
            pltpu.VMEM((88, LANES), jnp.float32),
            own, pltpu.VMEM((tiles * rows, lanes), jnp.bfloat16), own, own, own, own, own,
            dma((steps,)),
            dma((5,)),
            dma((3 + steps,)),
        ],
        compiler_params=pltpu.CompilerParams(vmem_limit_bytes=VMEM_LIMIT),
        name="finish",
    )(gathered.reshape(COPIES, OWN_ROWS, LANES), inverse, scales, *flat)
    shape = (tiles, rows, lanes)
    return master_new.reshape(shape), first_new.reshape(shape), second_new.reshape(shape), codes, rollout_scales


def solution(mesh):
    split = P("fsdp", "replica", None)
    return jax.shard_map(
        on_device,
        mesh=mesh,
        in_specs=(split, split, split, split, P()),
        out_specs=(split, split, split, P("fsdp", None, None), P("fsdp")),
        check_vma=False,
    )
```

```python
import functools

import jax
import jax.numpy as jnp
from jax import lax
from jax.experimental import pallas as pl
from jax.experimental.pallas import tpu as pltpu
from jax.sharding import PartitionSpec as P

MESH = pl.DeviceIdType.MESH

RB = 16
CB = 56
CAP_OWN = 84
HOLDERS = 32
COPIES = 16

RATE = 0.003
BETA_ONE = 0.9
BETA_TWO = 0.95
EPSILON = 1e-08
DECAY = 0.1
CORRECT_ONE = 0.99997343861
CORRECT_TWO = 0.99407947

ROWS = 8
LANES = 128
PER_PAIR = 6
OWN_ROWS = CAP_OWN * ROWS
PIECES = ((0, 256), (256, 256), (512, 160))
VMEM_LIMIT = 63 << 20
GROUP = 14
REACH = 22


def adam(master, gradient, first_moment, second_moment):
    grad_float = gradient.astype(jnp.float32)
    first_new = BETA_ONE * first_moment + (1.0 - BETA_ONE) * grad_float
    second_new = BETA_TWO * second_moment + (1.0 - BETA_TWO) * grad_float * grad_float
    direction = first_new / CORRECT_ONE / (jnp.sqrt(second_new / CORRECT_TWO) + EPSILON)
    master_new = master - RATE * (direction + DECAY * master)
    return master_new, first_new, second_new


def exchange(
    counts_ref, master_in, gradient_in, first_in, second_in,
    codes_out, scales_out, master_out, first_out, second_out,
    master_ref, gradient_ref, first_ref, second_ref, in_sem,
    all_ref, codes, inverse_ref, scales_ref, out_sem, raw, send, recv, own, peak, peak_z, peak_y, table,
    a2a_send, a2a_recv, peak_send, peak_recv, gather_send, z_near, z_far, y_near, y_far, local_sem,
):
    f = lax.axis_index("fsdp")
    rep = lax.axis_index("replica")
    zh, y = rep // 4, lax.rem(rep, 4)
    e, r = f // RB, lax.rem(f, RB)
    lowest = e * (HOLDERS - REACH)
    wide = (f >= HOLDERS - REACH) & (f < REACH)

    def at_z(step):
        return {"replica": lax.rem(zh + step + 4, 4) * 4 + y}

    def at_y(step):
        return {"replica": zh * 4 + lax.rem(y + step + 4, 4)}

    def at_f(step):
        return {"fsdp": lax.rem(f + step, HOLDERS)}

    inputs = ((master_in, master_ref), (gradient_in, gradient_ref), (first_in, first_ref), (second_in, second_ref))
    inputs = [pltpu.make_async_copy(source, target, in_sem.at[i]) for i, (source, target) in enumerate(inputs)]
    for copy in inputs:
        copy.start()
    barrier = pltpu.get_barrier_semaphore()

    def greet(step, carry):
        source = lax.rem(f + step, HOLDERS)

        @pl.when(((source < RB) & (f < REACH)) | ((source >= RB) & (f >= HOLDERS - REACH)))
        def _():
            pl.semaphore_signal(barrier, inc=1, device_id={"fsdp": source}, device_id_type=MESH)

        return carry

    lax.fori_loop(1, HOLDERS, greet, 0)
    for step in (1, 2, 3):
        pl.semaphore_signal(barrier, inc=1, device_id=at_z(step), device_id_type=MESH)
        pl.semaphore_signal(barrier, inc=1, device_id=at_y(step), device_id_type=MESH)

    lane = lax.broadcasted_iota(jnp.int32, (ROWS, LANES), 1)
    row = lax.broadcasted_iota(jnp.int32, (ROWS, LANES), 0)
    for copy in inputs:
        copy.wait()
    span = 8 * ROWS
    peaks = jnp.zeros((ROWS, LANES), jnp.float32)
    for step in range(CB // 8):
        here = pl.ds(step * span, span)
        master_new, first_new, second_new = adam(
            master_ref[here, :], gradient_ref[here, :], first_ref[here, :], second_ref[here, :]
        )
        master_ref[here, :] = master_new
        first_ref[here, :] = first_new
        second_ref[here, :] = second_new
        raw[here, :] = master_new.astype(jnp.bfloat16)
        tall = jnp.max(jnp.abs(master_new).reshape(8, ROWS, LANES), axis=1)
        peaks = jnp.where(lane == row + step * 8, jnp.max(tall, axis=1, keepdims=True), peaks)
    peak[...] = jnp.broadcast_to(jnp.max(peaks, axis=0, keepdims=True), (ROWS, LANES))

    begins = [jnp.int32(0)]
    for o in range(HOLDERS - 1):
        begins.append(begins[-1] + counts_ref[o])
    line = lax.broadcasted_iota(jnp.int32, (48, LANES), 0)
    column = lax.broadcasted_iota(jnp.int32, (48, LANES), 1)
    for i in range(REACH):
        begin = begins[i] + e * (begins[i + HOLDERS - REACH] - begins[i])
        first = ((jnp.full((48, LANES), begin, jnp.int32) - r + (RB - 1)) >> 4) - CB * e
        place = first * ROWS + line - column
        packed = jnp.zeros((48, LANES), jnp.float32)
        for low in range(0, CB * ROWS, LANES):
            width = min(LANES, CB * ROWS - low)
            ones = jnp.where(place == low, 1.0, 0.0).astype(jnp.bfloat16)[:, :width]
            packed += jnp.dot(ones, raw[pl.ds(low, width), :], preferred_element_type=jnp.float32)
        send[pl.ds(i * 48, 48), :] = packed.astype(jnp.bfloat16)
    for piece in range(3):
        mine = send[pl.ds(pl.multiple_of((f - lowest) * 48 + piece * 16, 16), 16), :]
        recv[pl.ds(pl.multiple_of(piece * 512 + f * 16, 16), 16), :] = mine

    begin = begins[HOLDERS - 1] * 0
    for o in range(1, HOLDERS):
        begin += jnp.where(f == o, 1, 0) * begins[o]
    start = jnp.full((ROWS, LANES), begin, jnp.int32)
    count = jnp.full((ROWS, LANES), counts_ref[f], jnp.int32)
    odd = [(start & (1 << bit)) != 0 for bit in range(4)]

    pl.semaphore_wait(barrier, REACH - 1 + 6)

    def owners(give):
        def visit(step, carry):
            i = lax.rem(f + step, REACH)

            @pl.when(lowest + i != f)
            def _():
                give(i)

            return carry

        lax.fori_loop(0, REACH, visit, 0)

    for piece in range(3):

        def give(i, piece=piece):
            pltpu.make_async_remote_copy(
                src_ref=send.at[pl.ds(pl.multiple_of(i * 48 + piece * 16, 16), 16)],
                dst_ref=recv.at[pl.ds(pl.multiple_of(piece * 512 + f * 16, 16), 16)],
                send_sem=a2a_send,
                recv_sem=a2a_recv.at[piece],
                device_id={"fsdp": lowest + i},
                device_id_type=MESH,
            ).start()

        owners(give)

    leaving = []

    def leave(source, target):
        copy = pltpu.make_async_copy(source, target, out_sem.at[len(leaving)])
        copy.start()
        leaving.append(copy)

    leave(master_ref, master_out)
    leave(first_ref, first_out)
    leave(second_ref, second_out)

    def tell(source, target, send_sem, recv_sem, device):
        copy = pltpu.make_async_remote_copy(
            src_ref=source, dst_ref=target, send_sem=send_sem, recv_sem=recv_sem, device_id=device, device_id_type=MESH
        )
        copy.start()

    def landed(target, sem):
        pltpu.make_async_copy(target, target, sem).wait()

    def landed_from_all(buffer, low, rows, sem):
        @pl.when(wide)
        def _():
            landed(buffer.at[pl.ds(low, (HOLDERS - 1) * rows)], sem)

        @pl.when(jnp.logical_not(wide))
        def _():
            landed(buffer.at[pl.ds(low, (RB - 1) * rows)], sem)

    for step in (1, 2, 3):
        tell(peak, peak_z.at[pl.ds((step - 1) * 8, 8)], peak_send.at[0], peak_recv.at[0], at_z(step))

    def order(piece):
        halves = [[], []]
        for r in range(RB):
            found = []
            for e in range(2):
                pair = recv[pl.ds(piece * 512 + (e * RB + r) * 16, 16), :]
                found.append(pair.astype(jnp.float32))
            position = start + ((r - start) & (RB - 1)) + piece * 32
            for half in range(2):
                here = slice(half * 8, half * 8 + 8)
                late = position >= RB * CB - half * 16
                halves[half].append(jnp.where(late, found[1][here, :], found[0][here, :]))
        for half in range(2):
            tiles = halves[half]
            for bit in range(4):
                tiles = [jnp.where(odd[bit], tiles[(k + (1 << bit)) % RB], tiles[k]) for k in range(RB)]
            slots = min(RB, PIECES[piece][1] // ROWS - half * RB)
            for k in range(0, slots, 2):
                both = jnp.concatenate([tiles[k], tiles[k + 1]], axis=0).astype(jnp.bfloat16)
                own[pl.ds((piece * 32 + half * 16 + k) * ROWS, 16), :] = both

    def chunk(z, yy, low, number):
        place = (z * 4 + yy) * OWN_ROWS + low
        return all_ref.at[pl.ds(pl.multiple_of(place, 16), number)]

    def z_at(step):
        return lax.rem(zh + step + 4, 4)

    def y_at(step):
        return lax.rem(y + step + 4, 4)

    def send_y(z_step, piece):
        low, number = PIECES[piece]
        place = chunk(z_at(z_step), y, low, number)
        source = own.at[pl.ds(low, number)] if z_step == 0 else place
        for way, step in enumerate((1, -1)):
            tell(source, place, gather_send, y_near.at[way, z_step, piece], at_y(step))

    locals_ = []
    for piece, (low, number) in enumerate(PIECES):
        landed_from_all(recv, piece * 512, 16, a2a_recv.at[piece])
        order(piece)
        here = own.at[pl.ds(low, number)]
        for way, step in enumerate((1, -1)):
            tell(here, chunk(zh, y, low, number), gather_send, z_near.at[way, piece], at_z(step))
        send_y(0, piece)
        keep = pltpu.make_async_copy(here, chunk(zh, y, low, number), local_sem.at[piece])
        keep.start()
        locals_.append(keep)

    def relay_z(piece):
        low, number = PIECES[piece]
        part = number // 2
        for way, step in enumerate((1, -1)):
            landed(chunk(z_at(-step), y, low, number), z_near.at[way, piece])
            half = chunk(z_at(-step), y, low + way * part, part)
            tell(half, half, gather_send, z_far.at[way, piece], at_z(step))
            send_y((-step) % 4, piece)

    def finish_z(piece):
        low, number = PIECES[piece]
        part = number // 2
        for way in range(2):
            landed(chunk(z_at(2), y, low + way * part, part), z_far.at[way, piece])
        send_y(2, piece)

    def relay_y(z_step, piece):
        low, number = PIECES[piece]
        part = number // 2
        for way, step in enumerate((1, -1)):
            landed(chunk(z_at(z_step), y_at(-step), low, number), y_near.at[way, z_step, piece])
            half = chunk(z_at(z_step), y_at(-step), low + way * part, part)
            tell(half, half, gather_send, y_far.at[way, z_step, piece], at_y(step))

    def peaks_y():
        landed(peak_z, peak_recv.at[0])
        landed(peak_z, peak_send.at[0])
        best = peak[...]
        for step in range(3):
            best = jnp.maximum(best, peak_z[pl.ds(step * 8, 8), :])
        peak[...] = best
        for step in (1, 2, 3):
            tell(peak, peak_y.at[pl.ds((step - 1) * 8, 8)], peak_send.at[1], peak_recv.at[1], at_y(step))

    def peaks_f():
        landed(peak_y, peak_recv.at[1])
        landed(peak_y, peak_send.at[1])
        best = peak[...]
        for step in range(3):
            best = jnp.maximum(best, peak_y[pl.ds(step * 8, 8), :])
        mine = table.at[pl.ds(pl.multiple_of(f * 8, 8), 8)]
        mine[...] = best

        def give(i):
            tell(mine, mine, peak_send.at[2], peak_recv.at[2], {"fsdp": lowest + i})

        owners(give)

    def scales():
        landed_from_all(table, 0, 8, peak_recv.at[2])
        landed(table.at[pl.ds(0, (REACH - 1) * 8)], peak_send.at[2])

        flat = jnp.zeros((ROWS, LANES), jnp.float32)
        for step in range(11):
            slot = step * 8 + row
            u = start + slot
            late = u >= RB * CB
            origin = (u & (RB - 1)) + jnp.where(late, RB, 0)
            found = jnp.zeros((ROWS, LANES), jnp.float32)
            for source in range(HOLDERS):
                found = jnp.where(origin == source, table[pl.ds(source * 8, 8), :], found)
            column = (u >> 4) - jnp.where(late, CB, 0)
            top = jnp.max(jnp.where(lane == column, found, 0.0), axis=1, keepdims=True)
            scale = jnp.broadcast_to((top + 1e-06).astype(jnp.bfloat16).astype(jnp.float32), (ROWS, LANES))
            filled = slot < count
            inverse_ref[pl.ds(step * 8, 8), :] = jnp.where(filled, 1.0 / scale, 0.0)
            flat = jnp.where((lane == slot) & filled, scale, flat)
        scales_ref[...] = jnp.max(flat, axis=0)[:CAP_OWN].astype(jnp.bfloat16)
        leave(scales_ref, scales_out)

    def code(z_step, piece):
        low, number = PIECES[piece]
        part = number // 2
        for way in range(2):
            landed(chunk(z_at(z_step), y_at(2), low + way * part, part), y_far.at[way, z_step, piece])
        if z_step == 0:
            locals_[piece].wait()
        first_slot, slots = low // ROWS, number // ROWS
        top = pl.multiple_of(z_at(z_step) * 32, 32)
        for base in range(first_slot, first_slot + slots, 8):
            count_here = min(8, first_slot + slots - base)
            factor = inverse_ref[pl.ds(base, count_here), :][:, None, :]
            for pair in range(2):
                parts = []
                for k in range(2):
                    place = (z_at(z_step) * 4 + pair * 2 + k) * OWN_ROWS + base * ROWS
                    tiles = all_ref[pl.ds(pl.multiple_of(place, 16), count_here * ROWS), :]
                    parts.append(tiles.astype(jnp.float32).reshape(count_here, ROWS, LANES))
                both = jnp.concatenate(parts, axis=1)
                coded = jnp.where(factor > 0.0, both * factor, 0.0).astype(jnp.bfloat16)
                codes[pl.ds(base, count_here), pl.ds(pl.multiple_of(top + pair * 16, 16), 16), :] = coded
        here = (pl.ds(first_slot, slots), pl.ds(top, 32))
        leave(codes.at[here], codes_out.at[here])

    relay_y(0, 0)
    relay_z(0)
    peaks_y()
    relay_y(0, 1)
    relay_z(1)
    relay_y(0, 2)
    peaks_f()
    relay_y(1, 0)
    relay_y(3, 0)
    finish_z(0)
    relay_z(2)
    relay_y(1, 1)
    relay_y(3, 1)
    finish_z(1)
    scales()
    code(0, 0)
    relay_y(2, 0)
    code(0, 1)
    code(0, 2)
    finish_z(2)
    relay_y(1, 2)
    relay_y(3, 2)
    code(3, 0)
    code(1, 0)
    relay_y(2, 1)
    code(3, 1)
    code(1, 1)
    relay_y(2, 2)
    code(2, 0)
    code(3, 2)
    code(1, 2)
    code(2, 1)
    code(2, 2)
    landed(send.at[pl.ds(0, (REACH - 1) * 48)], a2a_send)
    landed(all_ref.at[pl.ds(0, 15 * OWN_ROWS)], gather_send)
    for copy in leaving:
        copy.wait()


def finish(
    codes_ref, scales_ref, master_ref, first_ref, second_ref,
    codes_out, scales_out, master_out, first_out, second_out,
    codes, scales, master, first, second, in_sem, out_sem,
):
    ways = [(codes_ref.at[pl.ds(low, GROUP)], codes.at[pl.ds(low, GROUP)], codes_out.at[pl.ds(low, GROUP)]) for low in range(0, CAP_OWN, GROUP)]
    ways += [(master_ref, master, master_out), (first_ref, first, first_out), (second_ref, second, second_out)]
    ways += [(scales_ref, scales, scales_out)]
    into = [pltpu.make_async_copy(source, here, in_sem.at[i]) for i, (source, here, _) in enumerate(ways)]
    out = [pltpu.make_async_copy(here, target, out_sem.at[i]) for i, (_, here, target) in enumerate(ways)]
    for copy in into:
        copy.start()
    for arriving, leaving in zip(into, out):
        arriving.wait()
        leaving.start()
    for copy in out:
        copy.wait()


def on_device(master, gradient, first_moment, second_moment, owner_counts):
    tiles, rows, lanes = master.shape
    flat = [a.reshape(tiles * rows, lanes) for a in (master, gradient, first_moment, second_moment)]
    hbm = pl.BlockSpec(memory_space=pl.ANY)
    dma = pltpu.SemaphoreType.DMA
    part = jax.ShapeDtypeStruct((tiles * rows, lanes), jnp.float32)
    own = pltpu.VMEM((tiles * rows, lanes), jnp.float32)
    results = (
        jax.ShapeDtypeStruct((CAP_OWN, 128, 128), jnp.bfloat16),
        jax.ShapeDtypeStruct((CAP_OWN,), jnp.bfloat16),
        part, part, part,
    )
    found = pl.pallas_call(
        exchange,
        out_shape=results,
        in_specs=[pl.BlockSpec(memory_space=pltpu.SMEM)] + [hbm] * 4,
        out_specs=(hbm,) * 5,
        scratch_shapes=[
            own, pltpu.VMEM((tiles * rows, lanes), jnp.bfloat16), own, own,
            dma((4,)),
            pltpu.VMEM((COPIES * OWN_ROWS, LANES), jnp.bfloat16),
            pltpu.VMEM((CAP_OWN, 128, 128), jnp.bfloat16),
            pltpu.VMEM((88, LANES), jnp.float32),
            pltpu.VMEM((CAP_OWN,), jnp.bfloat16),
            dma((16,)),
            pltpu.VMEM((CB * ROWS, LANES), jnp.bfloat16),
            pltpu.VMEM((REACH * 48, LANES), jnp.bfloat16),
            pltpu.VMEM((3 * 512, LANES), jnp.bfloat16),
            pltpu.VMEM((OWN_ROWS, LANES), jnp.bfloat16),
            pltpu.VMEM((ROWS, LANES), jnp.float32),
            pltpu.VMEM((3 * ROWS, LANES), jnp.float32),
            pltpu.VMEM((3 * ROWS, LANES), jnp.float32),
            pltpu.VMEM((HOLDERS * ROWS, LANES), jnp.float32),
            dma,
            dma((3,)),
            dma((3,)),
            dma((3,)),
            dma,
            dma((2, 3)),
            dma((2, 3)),
            dma((2, 4, 3)),
            dma((2, 4, 3)),
            dma((3,)),
        ],
        compiler_params=pltpu.CompilerParams(collective_id=0, has_side_effects=True, vmem_limit_bytes=VMEM_LIMIT),
        name="exchange",
    )(owner_counts, *flat)
    codes, rollout_scales, master_new, first_new, second_new = pl.pallas_call(
        finish,
        out_shape=results,
        in_specs=[hbm] * 5,
        out_specs=(hbm,) * 5,
        scratch_shapes=[
            pltpu.VMEM((CAP_OWN, 128, 128), jnp.bfloat16),
            pltpu.VMEM((CAP_OWN,), jnp.bfloat16),
            own, own, own,
            dma((CAP_OWN // GROUP + 4,)),
            dma((CAP_OWN // GROUP + 4,)),
        ],
        compiler_params=pltpu.CompilerParams(vmem_limit_bytes=VMEM_LIMIT),
        name="finish",
    )(*found)
    shape = (tiles, rows, lanes)
    return master_new.reshape(shape), first_new.reshape(shape), second_new.reshape(shape), codes, rollout_scales


def solution(mesh):
    split = P("fsdp", "replica", None)
    return jax.shard_map(
        on_device,
        mesh=mesh,
        in_specs=(split, split, split, split, P()),
        out_specs=(split, split, split, P("fsdp", None, None), P("fsdp")),
        check_vma=False,
    )
```

```python
import functools

import jax
import jax.numpy as jnp
from jax import lax
from jax.experimental import pallas as pl
from jax.experimental.pallas import tpu as pltpu
from jax.sharding import PartitionSpec as P

MESH = pl.DeviceIdType.MESH

RB = 16
CB = 56
CAP_OWN = 84
HOLDERS = 32
COPIES = 16

RATE = 0.003
BETA_ONE = 0.9
BETA_TWO = 0.95
EPSILON = 1e-08
DECAY = 0.1
CORRECT_ONE = 0.99997343861
CORRECT_TWO = 0.99407947

ROWS = 8
LANES = 128
PER_PAIR = 6
OWN_ROWS = CAP_OWN * ROWS
ARRIVED = (32, 64, 84)
DIRECT = ()
PIECES = ((0, 32), (32, 192), (224, 448))
VMEM_LIMIT = 63 << 20
GROUP = 14
REACH = 22


ORDER = 'ry00 rz0 py ry01 rz1 ry02 pf ry10 ry30 fz0 rz2 ry11 ry31 fz1 sc co00 ry20 co01 co02 fz2 ry12 ry32 co30 co10 ry21 co31 co11 ry22 co20 co32 co12 co21 co22'


def adam(master, gradient, first_moment, second_moment):
    grad_float = gradient.astype(jnp.float32)
    first_new = BETA_ONE * first_moment + (1.0 - BETA_ONE) * grad_float
    second_new = BETA_TWO * second_moment + (1.0 - BETA_TWO) * grad_float * grad_float
    direction = first_new / CORRECT_ONE / (jnp.sqrt(second_new / CORRECT_TWO) + EPSILON)
    master_new = master - RATE * (direction + DECAY * master)
    return master_new, first_new, second_new


def exchange(
    counts_ref, master_in, gradient_in, first_in, second_in,
    codes_out, scales_out, master_out, first_out, second_out,
    master_ref, gradient_ref, first_ref, second_ref, in_sem,
    all_ref, codes, inverse_ref, scales_ref, out_sem, raw, send, recv, own, peak, peak_z, peak_y, table,
    a2a_send, a2a_recv, peak_send, peak_recv, gather_send, z_near, z_far, y_near, y_far, local_sem,
):
    f = lax.axis_index("fsdp")
    rep = lax.axis_index("replica")
    zh, y = rep // 4, lax.rem(rep, 4)
    e, r = f // RB, lax.rem(f, RB)
    lowest = e * (HOLDERS - REACH)
    wide = (f >= HOLDERS - REACH) & (f < REACH)

    def at_z(step):
        return {"replica": lax.rem(zh + step + 4, 4) * 4 + y}

    def at_y(step):
        return {"replica": zh * 4 + lax.rem(y + step + 4, 4)}

    def at_f(step):
        return {"fsdp": lax.rem(f + step, HOLDERS)}

    inputs = ((master_in, master_ref), (gradient_in, gradient_ref), (first_in, first_ref), (second_in, second_ref))
    inputs = [pltpu.make_async_copy(source, target, in_sem.at[i]) for i, (source, target) in enumerate(inputs)]
    for copy in inputs:
        copy.start()
    barrier = pltpu.get_barrier_semaphore()

    def greet(step, carry):
        source = lax.rem(f + step, HOLDERS)

        @pl.when(((source < RB) & (f < REACH)) | ((source >= RB) & (f >= HOLDERS - REACH)))
        def _():
            pl.semaphore_signal(barrier, inc=1, device_id={"fsdp": source}, device_id_type=MESH)

        return carry

    lax.fori_loop(1, HOLDERS, greet, 0)
    for step in (1, 2, 3):
        pl.semaphore_signal(barrier, inc=1, device_id=at_z(step), device_id_type=MESH)
        pl.semaphore_signal(barrier, inc=1, device_id=at_y(step), device_id_type=MESH)

    lane = lax.broadcasted_iota(jnp.int32, (ROWS, LANES), 1)
    row = lax.broadcasted_iota(jnp.int32, (ROWS, LANES), 0)
    for copy in inputs:
        copy.wait()
    span = 8 * ROWS
    peaks = jnp.zeros((ROWS, LANES), jnp.float32)
    for step in range(CB // 8):
        here = pl.ds(step * span, span)
        master_new, first_new, second_new = adam(
            master_ref[here, :], gradient_ref[here, :], first_ref[here, :], second_ref[here, :]
        )
        master_ref[here, :] = master_new
        first_ref[here, :] = first_new
        second_ref[here, :] = second_new
        raw[here, :] = master_new.astype(jnp.bfloat16)
        tall = jnp.max(jnp.abs(master_new).reshape(8, ROWS, LANES), axis=1)
        peaks = jnp.where(lane == row + step * 8, jnp.max(tall, axis=1, keepdims=True), peaks)
    peak[...] = jnp.broadcast_to(jnp.max(peaks, axis=0, keepdims=True), (ROWS, LANES))

    begins = [jnp.int32(0)]
    for o in range(HOLDERS - 1):
        begins.append(begins[-1] + counts_ref[o])
    line = lax.broadcasted_iota(jnp.int32, (48, LANES), 0)
    column = lax.broadcasted_iota(jnp.int32, (48, LANES), 1)
    for i in range(REACH):
        begin = begins[i] + e * (begins[i + HOLDERS - REACH] - begins[i])
        first = ((jnp.full((48, LANES), begin, jnp.int32) - r + (RB - 1)) >> 4) - CB * e
        place = first * ROWS + line - column
        packed = jnp.zeros((48, LANES), jnp.float32)
        for low in range(0, CB * ROWS, LANES):
            width = min(LANES, CB * ROWS - low)
            ones = jnp.where(place == low, 1.0, 0.0).astype(jnp.bfloat16)[:, :width]
            packed += jnp.dot(ones, raw[pl.ds(low, width), :], preferred_element_type=jnp.float32)
        send[pl.ds(i * 48, 48), :] = packed.astype(jnp.bfloat16)
    for piece in range(3):
        mine = send[pl.ds(pl.multiple_of((f - lowest) * 48 + piece * 16, 16), 16), :]
        recv[pl.ds(pl.multiple_of(piece * 512 + f * 16, 16), 16), :] = mine

    begin = begins[HOLDERS - 1] * 0
    for o in range(1, HOLDERS):
        begin += jnp.where(f == o, 1, 0) * begins[o]
    start = jnp.full((ROWS, LANES), begin, jnp.int32)
    count = jnp.full((ROWS, LANES), counts_ref[f], jnp.int32)
    odd = [(start & (1 << bit)) != 0 for bit in range(4)]

    pl.semaphore_wait(barrier, REACH - 1 + 6)

    def owners(give):
        def visit(step, carry):
            i = lax.rem(f + step, REACH)

            @pl.when(lowest + i != f)
            def _():
                give(i)

            return carry

        lax.fori_loop(0, REACH, visit, 0)

    for piece in range(3):

        def give(i, piece=piece):
            pltpu.make_async_remote_copy(
                src_ref=send.at[pl.ds(pl.multiple_of(i * 48 + piece * 16, 16), 16)],
                dst_ref=recv.at[pl.ds(pl.multiple_of(piece * 512 + f * 16, 16), 16)],
                send_sem=a2a_send,
                recv_sem=a2a_recv.at[piece],
                device_id={"fsdp": lowest + i},
                device_id_type=MESH,
            ).start()

        owners(give)

    leaving = []

    def leave(source, target):
        copy = pltpu.make_async_copy(source, target, out_sem.at[len(leaving)])
        copy.start()
        leaving.append(copy)

    leave(master_ref, master_out)
    leave(first_ref, first_out)
    leave(second_ref, second_out)

    def tell(source, target, send_sem, recv_sem, device):
        copy = pltpu.make_async_remote_copy(
            src_ref=source, dst_ref=target, send_sem=send_sem, recv_sem=recv_sem, device_id=device, device_id_type=MESH
        )
        copy.start()

    def landed(target, sem):
        pltpu.make_async_copy(target, target, sem).wait()

    def landed_from_all(buffer, low, rows, sem):
        @pl.when(wide)
        def _():
            landed(buffer.at[pl.ds(low, (HOLDERS - 1) * rows)], sem)

        @pl.when(jnp.logical_not(wide))
        def _():
            landed(buffer.at[pl.ds(low, (RB - 1) * rows)], sem)

    for step in (1, 2, 3):
        tell(peak, peak_z.at[pl.ds((step - 1) * 8, 8)], peak_send.at[0], peak_recv.at[0], at_z(step))

    def order(piece):
        halves = [[], []]
        for r in range(RB):
            found = []
            for e in range(2):
                pair = recv[pl.ds(piece * 512 + (e * RB + r) * 16, 16), :]
                found.append(pair.astype(jnp.float32))
            position = start + ((r - start) & (RB - 1)) + piece * 32
            for half in range(2):
                here = slice(half * 8, half * 8 + 8)
                late = position >= RB * CB - half * 16
                halves[half].append(jnp.where(late, found[1][here, :], found[0][here, :]))
        for half in range(2):
            tiles = halves[half]
            for bit in range(4):
                tiles = [jnp.where(odd[bit], tiles[(k + (1 << bit)) % RB], tiles[k]) for k in range(RB)]
            slots = min(RB, ARRIVED[piece] - piece * 32 - half * RB)
            for k in range(0, slots, 2):
                both = jnp.concatenate([tiles[k], tiles[k + 1]], axis=0).astype(jnp.bfloat16)
                own[pl.ds((piece * 32 + half * 16 + k) * ROWS, 16), :] = both

    def chunk(z, yy, low, number):
        place = (z * 4 + yy) * OWN_ROWS + low
        return all_ref.at[pl.ds(pl.multiple_of(place, 16), number)]

    def z_at(step):
        return lax.rem(zh + step + 4, 4)

    def y_at(step):
        return lax.rem(y + step + 4, 4)

    def send_y(z_step, piece):
        low, number = PIECES[piece]
        place = chunk(z_at(z_step), y, low, number)
        source = own.at[pl.ds(low, number)] if z_step == 0 else place
        for way, step in enumerate((1, -1)):
            tell(source, place, gather_send, y_near.at[way, z_step, piece], at_y(step))
        if (z_step, piece) in DIRECT:
            tell(source, place, gather_send, y_far.at[0, z_step, piece], at_y(2))

    locals_ = []
    for part in range(3):
        landed_from_all(recv, part * 512, 16, a2a_recv.at[part])
        order(part)
        for piece, (low, number) in enumerate(PIECES):
            if piece == len(locals_) and low + number <= ARRIVED[part] * ROWS:
                here = own.at[pl.ds(low, number)]
                for way, step in enumerate((1, -1)):
                    tell(here, chunk(zh, y, low, number), gather_send, z_near.at[way, piece], at_z(step))
                send_y(0, piece)
                keep = pltpu.make_async_copy(here, chunk(zh, y, low, number), local_sem.at[piece])
                keep.start()
                locals_.append(keep)

    def relay_z(piece):
        low, number = PIECES[piece]
        part = number // 2
        for way, step in enumerate((1, -1)):
            landed(chunk(z_at(-step), y, low, number), z_near.at[way, piece])
            half = chunk(z_at(-step), y, low + way * part, part)
            tell(half, half, gather_send, z_far.at[way, piece], at_z(step))
            send_y((-step) % 4, piece)

    def finish_z(piece):
        low, number = PIECES[piece]
        part = number // 2
        for way in range(2):
            landed(chunk(z_at(2), y, low + way * part, part), z_far.at[way, piece])
        send_y(2, piece)

    def relay_y(z_step, piece):
        low, number = PIECES[piece]
        part = number // 2
        for way, step in enumerate((1, -1)):
            landed(chunk(z_at(z_step), y_at(-step), low, number), y_near.at[way, z_step, piece])
            if (z_step, piece) in DIRECT:
                continue
            half = chunk(z_at(z_step), y_at(-step), low + way * part, part)
            tell(half, half, gather_send, y_far.at[way, z_step, piece], at_y(step))

    def peaks_y():
        landed(peak_z, peak_recv.at[0])
        landed(peak_z, peak_send.at[0])
        best = peak[...]
        for step in range(3):
            best = jnp.maximum(best, peak_z[pl.ds(step * 8, 8), :])
        peak[...] = best
        for step in (1, 2, 3):
            tell(peak, peak_y.at[pl.ds((step - 1) * 8, 8)], peak_send.at[1], peak_recv.at[1], at_y(step))

    def peaks_f():
        landed(peak_y, peak_recv.at[1])
        landed(peak_y, peak_send.at[1])
        best = peak[...]
        for step in range(3):
            best = jnp.maximum(best, peak_y[pl.ds(step * 8, 8), :])
        mine = table.at[pl.ds(pl.multiple_of(f * 8, 8), 8)]
        mine[...] = best

        def give(i):
            tell(mine, mine, peak_send.at[2], peak_recv.at[2], {"fsdp": lowest + i})

        owners(give)

    def scales():
        landed_from_all(table, 0, 8, peak_recv.at[2])
        landed(table.at[pl.ds(0, (REACH - 1) * 8)], peak_send.at[2])

        flat = jnp.zeros((ROWS, LANES), jnp.float32)
        for step in range(11):
            slot = step * 8 + row
            u = start + slot
            late = u >= RB * CB
            origin = (u & (RB - 1)) + jnp.where(late, RB, 0)
            found = jnp.zeros((ROWS, LANES), jnp.float32)
            for source in range(HOLDERS):
                found = jnp.where(origin == source, table[pl.ds(source * 8, 8), :], found)
            column = (u >> 4) - jnp.where(late, CB, 0)
            top = jnp.max(jnp.where(lane == column, found, 0.0), axis=1, keepdims=True)
            scale = jnp.broadcast_to((top + 1e-06).astype(jnp.bfloat16).astype(jnp.float32), (ROWS, LANES))
            filled = slot < count
            inverse_ref[pl.ds(step * 8, 8), :] = jnp.where(filled, 1.0 / scale, 0.0)
            flat = jnp.where((lane == slot) & filled, scale, flat)
        scales_ref[...] = jnp.max(flat, axis=0)[:CAP_OWN].astype(jnp.bfloat16)
        leave(scales_ref, scales_out)

    def code(z_step, piece):
        low, number = PIECES[piece]
        part = number // 2
        if (z_step, piece) in DIRECT:
            landed(chunk(z_at(z_step), y_at(2), low, number), y_far.at[0, z_step, piece])
        else:
            for way in range(2):
                landed(chunk(z_at(z_step), y_at(2), low + way * part, part), y_far.at[way, z_step, piece])
        if z_step == 0:
            locals_[piece].wait()
        first_slot, slots = low // ROWS, number // ROWS
        top = pl.multiple_of(z_at(z_step) * 32, 32)
        for base in range(first_slot, first_slot + slots, 8):
            count_here = min(8, first_slot + slots - base)
            factor = inverse_ref[pl.ds(base, count_here), :][:, None, :]
            for pair in range(2):
                parts = []
                for k in range(2):
                    place = (z_at(z_step) * 4 + pair * 2 + k) * OWN_ROWS + base * ROWS
                    tiles = all_ref[pl.ds(pl.multiple_of(place, 16), count_here * ROWS), :]
                    parts.append(tiles.astype(jnp.float32).reshape(count_here, ROWS, LANES))
                both = jnp.concatenate(parts, axis=1)
                coded = jnp.where(factor > 0.0, both * factor, 0.0).astype(jnp.bfloat16)
                codes[pl.ds(base, count_here), pl.ds(pl.multiple_of(top + pair * 16, 16), 16), :] = coded
        here = (pl.ds(first_slot, slots), pl.ds(top, 32))
        leave(codes.at[here], codes_out.at[here])

    tasks = dict(
        ry=relay_y, rz=relay_z, fz=finish_z, co=code, py=peaks_y, pf=peaks_f, sc=scales,
    )
    for task in ORDER.split():
        tasks[task[:2]](*[int(digit) for digit in task[2:]])
    landed(send.at[pl.ds(0, (REACH - 1) * 48)], a2a_send)
    landed(all_ref.at[pl.ds(0, 15 * OWN_ROWS)], gather_send)
    for copy in leaving:
        copy.wait()


def finish(
    codes_ref, scales_ref, master_ref, first_ref, second_ref,
    codes_out, scales_out, master_out, first_out, second_out,
    codes, scales, master, first, second, in_sem, out_sem,
):
    ways = [(codes_ref.at[pl.ds(low, GROUP)], codes.at[pl.ds(low, GROUP)], codes_out.at[pl.ds(low, GROUP)]) for low in range(0, CAP_OWN, GROUP)]
    ways += [(master_ref, master, master_out), (first_ref, first, first_out), (second_ref, second, second_out)]
    ways += [(scales_ref, scales, scales_out)]
    into = [pltpu.make_async_copy(source, here, in_sem.at[i]) for i, (source, here, _) in enumerate(ways)]
    out = [pltpu.make_async_copy(here, target, out_sem.at[i]) for i, (_, here, target) in enumerate(ways)]
    for copy in into:
        copy.start()
    for arriving, leaving in zip(into, out):
        arriving.wait()
        leaving.start()
    for copy in out:
        copy.wait()


def on_device(master, gradient, first_moment, second_moment, owner_counts):
    tiles, rows, lanes = master.shape
    flat = [a.reshape(tiles * rows, lanes) for a in (master, gradient, first_moment, second_moment)]
    hbm = pl.BlockSpec(memory_space=pl.ANY)
    dma = pltpu.SemaphoreType.DMA
    part = jax.ShapeDtypeStruct((tiles * rows, lanes), jnp.float32)
    own = pltpu.VMEM((tiles * rows, lanes), jnp.float32)
    results = (
        jax.ShapeDtypeStruct((CAP_OWN, 128, 128), jnp.bfloat16),
        jax.ShapeDtypeStruct((CAP_OWN,), jnp.bfloat16),
        part, part, part,
    )
    found = pl.pallas_call(
        exchange,
        out_shape=results,
        in_specs=[pl.BlockSpec(memory_space=pltpu.SMEM)] + [hbm] * 4,
        out_specs=(hbm,) * 5,
        scratch_shapes=[
            own, pltpu.VMEM((tiles * rows, lanes), jnp.bfloat16), own, own,
            dma((4,)),
            pltpu.VMEM((COPIES * OWN_ROWS, LANES), jnp.bfloat16),
            pltpu.VMEM((CAP_OWN, 128, 128), jnp.bfloat16),
            pltpu.VMEM((88, LANES), jnp.float32),
            pltpu.VMEM((CAP_OWN,), jnp.bfloat16),
            dma((4 + 4 * len(PIECES),)),
            pltpu.VMEM((CB * ROWS, LANES), jnp.bfloat16),
            pltpu.VMEM((REACH * 48, LANES), jnp.bfloat16),
            pltpu.VMEM((3 * 512, LANES), jnp.bfloat16),
            pltpu.VMEM((OWN_ROWS, LANES), jnp.bfloat16),
            pltpu.VMEM((ROWS, LANES), jnp.float32),
            pltpu.VMEM((3 * ROWS, LANES), jnp.float32),
            pltpu.VMEM((3 * ROWS, LANES), jnp.float32),
            pltpu.VMEM((HOLDERS * ROWS, LANES), jnp.float32),
            dma,
            dma((3,)),
            dma((3,)),
            dma((3,)),
            dma,
            dma((2, len(PIECES))),
            dma((2, len(PIECES))),
            dma((2, 4, len(PIECES))),
            dma((2, 4, len(PIECES))),
            dma((len(PIECES),)),
        ],
        compiler_params=pltpu.CompilerParams(collective_id=0, has_side_effects=True, vmem_limit_bytes=VMEM_LIMIT),
        name="exchange",
    )(owner_counts, *flat)
    codes, rollout_scales, master_new, first_new, second_new = pl.pallas_call(
        finish,
        out_shape=results,
        in_specs=[hbm] * 5,
        out_specs=(hbm,) * 5,
        scratch_shapes=[
            pltpu.VMEM((CAP_OWN, 128, 128), jnp.bfloat16),
            pltpu.VMEM((CAP_OWN,), jnp.bfloat16),
            own, own, own,
            dma((CAP_OWN // GROUP + 4,)),
            dma((CAP_OWN // GROUP + 4,)),
        ],
        compiler_params=pltpu.CompilerParams(vmem_limit_bytes=VMEM_LIMIT),
        name="finish",
    )(*found)
    shape = (tiles, rows, lanes)
    return master_new.reshape(shape), first_new.reshape(shape), second_new.reshape(shape), codes, rollout_scales


def solution(mesh):
    split = P("fsdp", "replica", None)
    return jax.shard_map(
        on_device,
        mesh=mesh,
        in_specs=(split, split, split, split, P()),
        out_specs=(split, split, split, P("fsdp", None, None), P("fsdp")),
        check_vma=False,
    )
```

```python
import functools

import jax
import jax.numpy as jnp
from jax import lax
from jax.experimental import pallas as pl
from jax.experimental.pallas import tpu as pltpu
from jax.sharding import PartitionSpec as P

MESH = pl.DeviceIdType.MESH

RB = 16
CB = 56
CAP_OWN = 84
HOLDERS = 32
COPIES = 16

RATE = 0.003
BETA_ONE = 0.9
BETA_TWO = 0.95
EPSILON = 1e-08
DECAY = 0.1
CORRECT_ONE = 0.99997343861
CORRECT_TWO = 0.99407947

ROWS = 8
LANES = 128
PER_PAIR = 6
OWN_ROWS = CAP_OWN * ROWS
ARRIVED = (32, 64, 84)
DIRECT = ()
PIECES = ((0, 32), (32, 192), (224, 448))
VMEM_LIMIT = 63 << 20
GROUP = 14
REACH = 22


ORDER = 'ry00 rz0 py ry01 rz1 ry02 pf ry10 ry30 fz0 rz2 ry11 ry31 fz1 sc co00 ry20 co01 co02 fz2 ry12 ry32 co30 co10 ry21 co31 co11 ry22 co20 co32 co12 co21 co22'


def adam(master, gradient, first_moment, second_moment):
    grad_float = gradient.astype(jnp.float32)
    first_new = BETA_ONE * first_moment + (1.0 - BETA_ONE) * grad_float
    second_new = BETA_TWO * second_moment + (1.0 - BETA_TWO) * grad_float * grad_float
    direction = first_new / CORRECT_ONE / (jnp.sqrt(second_new / CORRECT_TWO) + EPSILON)
    master_new = master - RATE * (direction + DECAY * master)
    return master_new, first_new, second_new


def exchange(
    counts_ref, master_in, gradient_in, first_in, second_in,
    codes_out, scales_out, master_out, first_out, second_out,
    master_ref, gradient_ref, first_ref, second_ref, in_sem,
    all_ref, codes, inverse_ref, scales_ref, out_sem, raw, send, recv, own, peak, peak_z, peak_y, table,
    a2a_send, a2a_recv, peak_send, peak_recv, gather_send, z_near, z_far, y_near, y_far, local_sem,
):
    f = lax.axis_index("fsdp")
    rep = lax.axis_index("replica")
    zh, y = rep // 4, lax.rem(rep, 4)
    e, r = f // RB, lax.rem(f, RB)
    lowest = e * (HOLDERS - REACH)
    wide = (f >= HOLDERS - REACH) & (f < REACH)

    def at_z(step):
        return {"replica": lax.rem(zh + step + 4, 4) * 4 + y}

    def at_y(step):
        return {"replica": zh * 4 + lax.rem(y + step + 4, 4)}

    def at_f(step):
        return {"fsdp": lax.rem(f + step, HOLDERS)}

    inputs = ((master_in, master_ref), (gradient_in, gradient_ref), (first_in, first_ref), (second_in, second_ref))
    inputs = [pltpu.make_async_copy(source, target, in_sem.at[i]) for i, (source, target) in enumerate(inputs)]
    for copy in inputs:
        copy.start()
    barrier = pltpu.get_barrier_semaphore()

    def greet(step, carry):
        source = lax.rem(f + step, HOLDERS)

        @pl.when(((source < RB) & (f < REACH)) | ((source >= RB) & (f >= HOLDERS - REACH)))
        def _():
            pl.semaphore_signal(barrier, inc=1, device_id={"fsdp": source}, device_id_type=MESH)

        return carry

    lax.fori_loop(1, HOLDERS, greet, 0)
    for step in (1, 2, 3):
        pl.semaphore_signal(barrier, inc=1, device_id=at_z(step), device_id_type=MESH)
        pl.semaphore_signal(barrier, inc=1, device_id=at_y(step), device_id_type=MESH)

    lane = lax.broadcasted_iota(jnp.int32, (ROWS, LANES), 1)
    row = lax.broadcasted_iota(jnp.int32, (ROWS, LANES), 0)
    for copy in inputs:
        copy.wait()
    span = 8 * ROWS
    peaks = jnp.zeros((ROWS, LANES), jnp.float32)
    for step in range(CB // 8):
        here = pl.ds(step * span, span)
        master_new, first_new, second_new = adam(
            master_ref[here, :], gradient_ref[here, :], first_ref[here, :], second_ref[here, :]
        )
        master_ref[here, :] = master_new
        first_ref[here, :] = first_new
        second_ref[here, :] = second_new
        raw[here, :] = master_new.astype(jnp.bfloat16)
        tall = jnp.max(jnp.abs(master_new).reshape(8, ROWS, LANES), axis=1)
        peaks = jnp.where(lane == row + step * 8, jnp.max(tall, axis=1, keepdims=True), peaks)
    peak[...] = jnp.broadcast_to(jnp.max(peaks, axis=0, keepdims=True), (ROWS, LANES))

    begins = [jnp.int32(0)]
    for o in range(HOLDERS - 1):
        begins.append(begins[-1] + counts_ref[o])
    line = lax.broadcasted_iota(jnp.int32, (48, LANES), 0)
    column = lax.broadcasted_iota(jnp.int32, (48, LANES), 1)
    for i in range(REACH):
        begin = begins[i] + e * (begins[i + HOLDERS - REACH] - begins[i])
        first = ((jnp.full((48, LANES), begin, jnp.int32) - r + (RB - 1)) >> 4) - CB * e
        place = first * ROWS + line - column
        packed = jnp.zeros((48, LANES), jnp.float32)
        for low in range(0, CB * ROWS, LANES):
            width = min(LANES, CB * ROWS - low)
            ones = jnp.where(place == low, 1.0, 0.0).astype(jnp.bfloat16)[:, :width]
            packed += jnp.dot(ones, raw[pl.ds(low, width), :], preferred_element_type=jnp.float32)
        send[pl.ds(i * 48, 48), :] = packed.astype(jnp.bfloat16)
    for piece in range(3):
        mine = send[pl.ds(pl.multiple_of((f - lowest) * 48 + piece * 16, 16), 16), :]
        recv[pl.ds(pl.multiple_of(piece * 512 + f * 16, 16), 16), :] = mine

    begin = begins[HOLDERS - 1] * 0
    for o in range(1, HOLDERS):
        begin += jnp.where(f == o, 1, 0) * begins[o]
    start = jnp.full((ROWS, LANES), begin, jnp.int32)
    count = jnp.full((ROWS, LANES), counts_ref[f], jnp.int32)
    odd = [(start & (1 << bit)) != 0 for bit in range(4)]

    pl.semaphore_wait(barrier, REACH - 1 + 6)

    def owners(give):
        def visit(step, carry):
            i = lax.rem(f + step, REACH)

            @pl.when(lowest + i != f)
            def _():
                give(i)

            return carry

        lax.fori_loop(0, REACH, visit, 0)

    for piece in range(3):

        def give(i, piece=piece):
            pltpu.make_async_remote_copy(
                src_ref=send.at[pl.ds(pl.multiple_of(i * 48 + piece * 16, 16), 16)],
                dst_ref=recv.at[pl.ds(pl.multiple_of(piece * 512 + f * 16, 16), 16)],
                send_sem=a2a_send,
                recv_sem=a2a_recv.at[piece],
                device_id={"fsdp": lowest + i},
                device_id_type=MESH,
            ).start()

        owners(give)

    leaving = []

    def leave(source, target):
        copy = pltpu.make_async_copy(source, target, out_sem.at[len(leaving)])
        copy.start()
        leaving.append(copy)

    leave(master_ref, master_out)
    leave(first_ref, first_out)
    leave(second_ref, second_out)

    def tell(source, target, send_sem, recv_sem, device):
        copy = pltpu.make_async_remote_copy(
            src_ref=source, dst_ref=target, send_sem=send_sem, recv_sem=recv_sem, device_id=device, device_id_type=MESH
        )
        copy.start()

    def landed(target, sem):
        pltpu.make_async_copy(target, target, sem).wait()

    def landed_from_all(buffer, low, rows, sem):
        @pl.when(wide)
        def _():
            landed(buffer.at[pl.ds(low, (HOLDERS - 1) * rows)], sem)

        @pl.when(jnp.logical_not(wide))
        def _():
            landed(buffer.at[pl.ds(low, (RB - 1) * rows)], sem)

    for step in (1, 2, 3):
        tell(peak, peak_z.at[pl.ds((step - 1) * 8, 8)], peak_send.at[0], peak_recv.at[0], at_z(step))

    def order(piece):
        halves = [[], []]
        for r in range(RB):
            found = []
            for e in range(2):
                pair = recv[pl.ds(piece * 512 + (e * RB + r) * 16, 16), :]
                found.append(pair.astype(jnp.float32))
            position = start + ((r - start) & (RB - 1)) + piece * 32
            for half in range(2):
                here = slice(half * 8, half * 8 + 8)
                late = position >= RB * CB - half * 16
                halves[half].append(jnp.where(late, found[1][here, :], found[0][here, :]))
        for half in range(2):
            tiles = halves[half]
            for bit in range(4):
                tiles = [jnp.where(odd[bit], tiles[(k + (1 << bit)) % RB], tiles[k]) for k in range(RB)]
            slots = min(RB, ARRIVED[piece] - piece * 32 - half * RB)
            for k in range(0, slots, 2):
                both = jnp.concatenate([tiles[k], tiles[k + 1]], axis=0).astype(jnp.bfloat16)
                own[pl.ds((piece * 32 + half * 16 + k) * ROWS, 16), :] = both

    def chunk(z, yy, low, number):
        place = (z * 4 + yy) * OWN_ROWS + low
        return all_ref.at[pl.ds(pl.multiple_of(place, 16), number)]

    def z_at(step):
        return lax.rem(zh + step + 4, 4)

    def y_at(step):
        return lax.rem(y + step + 4, 4)

    def send_y(z_step, piece):
        low, number = PIECES[piece]
        place = chunk(z_at(z_step), y, low, number)
        source = own.at[pl.ds(low, number)] if z_step == 0 else place
        for way, step in enumerate((1, -1)):
            tell(source, place, gather_send, y_near.at[way, z_step, piece], at_y(step))
        if (z_step, piece) in DIRECT:
            tell(source, place, gather_send, y_far.at[0, z_step, piece], at_y(2))

    locals_ = []
    for part in range(3):
        landed_from_all(recv, part * 512, 16, a2a_recv.at[part])
        order(part)
        for piece, (low, number) in enumerate(PIECES):
            if piece == len(locals_) and low + number <= ARRIVED[part] * ROWS:
                here = own.at[pl.ds(low, number)]
                for way, step in enumerate((1, -1)):
                    tell(here, chunk(zh, y, low, number), gather_send, z_near.at[way, piece], at_z(step))
                send_y(0, piece)
                keep = pltpu.make_async_copy(here, chunk(zh, y, low, number), local_sem.at[piece])
                keep.start()
                locals_.append(keep)

    def relay_z(piece):
        low, number = PIECES[piece]
        part = number // 2
        for way, step in enumerate((1, -1)):
            landed(chunk(z_at(-step), y, low, number), z_near.at[way, piece])
            half = chunk(z_at(-step), y, low + way * part, part)
            tell(half, half, gather_send, z_far.at[way, piece], at_z(step))
            send_y((-step) % 4, piece)

    def finish_z(piece):
        low, number = PIECES[piece]
        part = number // 2
        for way in range(2):
            landed(chunk(z_at(2), y, low + way * part, part), z_far.at[way, piece])
        send_y(2, piece)

    def relay_y(z_step, piece):
        low, number = PIECES[piece]
        part = number // 2
        for way, step in enumerate((1, -1)):
            landed(chunk(z_at(z_step), y_at(-step), low, number), y_near.at[way, z_step, piece])
            if (z_step, piece) in DIRECT:
                continue
            half = chunk(z_at(z_step), y_at(-step), low + way * part, part)
            tell(half, half, gather_send, y_far.at[way, z_step, piece], at_y(step))

    def peaks_y():
        landed(peak_z, peak_recv.at[0])
        landed(peak_z, peak_send.at[0])
        best = peak[...]
        for step in range(3):
            best = jnp.maximum(best, peak_z[pl.ds(step * 8, 8), :])
        peak[...] = best
        for step in (1, 2, 3):
            tell(peak, peak_y.at[pl.ds((step - 1) * 8, 8)], peak_send.at[1], peak_recv.at[1], at_y(step))

    def peaks_f():
        landed(peak_y, peak_recv.at[1])
        landed(peak_y, peak_send.at[1])
        best = peak[...]
        for step in range(3):
            best = jnp.maximum(best, peak_y[pl.ds(step * 8, 8), :])
        mine = table.at[pl.ds(pl.multiple_of(f * 8, 8), 8)]
        mine[...] = best

        def give(i):
            tell(mine, mine, peak_send.at[2], peak_recv.at[2], {"fsdp": lowest + i})

        owners(give)

    def scales():
        landed_from_all(table, 0, 8, peak_recv.at[2])
        landed(table.at[pl.ds(0, (REACH - 1) * 8)], peak_send.at[2])

        flat = jnp.zeros((ROWS, LANES), jnp.float32)
        for step in range(11):
            slot = step * 8 + row
            u = start + slot
            late = u >= RB * CB
            origin = (u & (RB - 1)) + jnp.where(late, RB, 0)
            found = jnp.zeros((ROWS, LANES), jnp.float32)
            for source in range(HOLDERS):
                found = jnp.where(origin == source, table[pl.ds(source * 8, 8), :], found)
            column = (u >> 4) - jnp.where(late, CB, 0)
            top = jnp.max(jnp.where(lane == column, found, 0.0), axis=1, keepdims=True)
            scale = jnp.broadcast_to((top + 1e-06).astype(jnp.bfloat16).astype(jnp.float32), (ROWS, LANES))
            filled = slot < count
            inverse_ref[pl.ds(step * 8, 8), :] = jnp.where(filled, 1.0 / scale, 0.0)
            flat = jnp.where((lane == slot) & filled, scale, flat)
        scales_ref[...] = jnp.max(flat, axis=0)[:CAP_OWN].astype(jnp.bfloat16)
        leave(scales_ref, scales_out)

    def code(z_step, piece):
        low, number = PIECES[piece]
        part = number // 2
        if (z_step, piece) in DIRECT:
            landed(chunk(z_at(z_step), y_at(2), low, number), y_far.at[0, z_step, piece])
        else:
            for way in range(2):
                landed(chunk(z_at(z_step), y_at(2), low + way * part, part), y_far.at[way, z_step, piece])
        if z_step == 0:
            locals_[piece].wait()
        first_slot, slots = low // ROWS, number // ROWS
        top = pl.multiple_of(z_at(z_step) * 32, 32)
        for base in range(first_slot, first_slot + slots, 8):
            count_here = min(8, first_slot + slots - base)
            factor = inverse_ref[pl.ds(base, count_here), :][:, None, :]
            for pair in range(2):
                parts = []
                for k in range(2):
                    place = (z_at(z_step) * 4 + pair * 2 + k) * OWN_ROWS + base * ROWS
                    tiles = all_ref[pl.ds(pl.multiple_of(place, 16), count_here * ROWS), :]
                    parts.append(tiles.astype(jnp.float32).reshape(count_here, ROWS, LANES))
                both = jnp.concatenate(parts, axis=1)
                coded = jnp.where(factor > 0.0, both * factor, 0.0).astype(jnp.bfloat16)
                codes[pl.ds(base, count_here), pl.ds(pl.multiple_of(top + pair * 16, 16), 16), :] = coded
        here = (pl.ds(first_slot, slots), pl.ds(top, 32))
        leave(codes.at[here], codes_out.at[here])

    tasks = dict(
        ry=relay_y, rz=relay_z, fz=finish_z, co=code, py=peaks_y, pf=peaks_f, sc=scales,
    )
    for task in ORDER.split():
        tasks[task[:2]](*[int(digit) for digit in task[2:]])
    landed(send.at[pl.ds(0, (REACH - 1) * 48)], a2a_send)
    landed(all_ref.at[pl.ds(0, 15 * OWN_ROWS)], gather_send)
    for copy in leaving:
        copy.wait()


def finish(
    codes_ref, scales_ref, master_ref, first_ref, second_ref,
    codes_out, scales_out, master_out, first_out, second_out,
    codes, scales, master, first, second, in_sem, out_sem,
):
    ways = [(scales_ref, scales, scales_out)]
    ways += [(master_ref, master, master_out), (first_ref, first, first_out), (second_ref, second, second_out)]
    for low in range(0, CAP_OWN, GROUP):
        part = pl.ds(low, GROUP)
        ways.append((codes_ref.at[part], codes.at[part], codes_out.at[part]))
    into = [pltpu.make_async_copy(source, here, in_sem.at[i]) for i, (source, here, _) in enumerate(ways)]
    out = [pltpu.make_async_copy(here, target, out_sem.at[i]) for i, (_, here, target) in enumerate(ways)]
    for copy in into:
        copy.start()
    for arriving, leaving in zip(into, out):
        arriving.wait()
        leaving.start()
    for copy in out:
        copy.wait()


def on_device(master, gradient, first_moment, second_moment, owner_counts):
    tiles, rows, lanes = master.shape
    flat = [a.reshape(tiles * rows, lanes) for a in (master, gradient, first_moment, second_moment)]
    hbm = pl.BlockSpec(memory_space=pl.ANY)
    dma = pltpu.SemaphoreType.DMA
    part = jax.ShapeDtypeStruct((tiles * rows, lanes), jnp.float32)
    own = pltpu.VMEM((tiles * rows, lanes), jnp.float32)
    results = (
        jax.ShapeDtypeStruct((CAP_OWN, 128, 128), jnp.bfloat16),
        jax.ShapeDtypeStruct((CAP_OWN,), jnp.bfloat16),
        part, part, part,
    )
    found = pl.pallas_call(
        exchange,
        out_shape=results,
        in_specs=[pl.BlockSpec(memory_space=pltpu.SMEM)] + [hbm] * 4,
        out_specs=(hbm,) * 5,
        scratch_shapes=[
            own, pltpu.VMEM((tiles * rows, lanes), jnp.bfloat16), own, own,
            dma((4,)),
            pltpu.VMEM((COPIES * OWN_ROWS, LANES), jnp.bfloat16),
            pltpu.VMEM((CAP_OWN, 128, 128), jnp.bfloat16),
            pltpu.VMEM((88, LANES), jnp.float32),
            pltpu.VMEM((CAP_OWN,), jnp.bfloat16),
            dma((4 + 4 * len(PIECES),)),
            pltpu.VMEM((CB * ROWS, LANES), jnp.bfloat16),
            pltpu.VMEM((REACH * 48, LANES), jnp.bfloat16),
            pltpu.VMEM((3 * 512, LANES), jnp.bfloat16),
            pltpu.VMEM((OWN_ROWS, LANES), jnp.bfloat16),
            pltpu.VMEM((ROWS, LANES), jnp.float32),
            pltpu.VMEM((3 * ROWS, LANES), jnp.float32),
            pltpu.VMEM((3 * ROWS, LANES), jnp.float32),
            pltpu.VMEM((HOLDERS * ROWS, LANES), jnp.float32),
            dma,
            dma((3,)),
            dma((3,)),
            dma((3,)),
            dma,
            dma((2, len(PIECES))),
            dma((2, len(PIECES))),
            dma((2, 4, len(PIECES))),
            dma((2, 4, len(PIECES))),
            dma((len(PIECES),)),
        ],
        compiler_params=pltpu.CompilerParams(collective_id=0, has_side_effects=True, vmem_limit_bytes=VMEM_LIMIT),
        name="exchange",
    )(owner_counts, *flat)
    codes, rollout_scales, master_new, first_new, second_new = pl.pallas_call(
        finish,
        out_shape=results,
        in_specs=[hbm] * 5,
        out_specs=(hbm,) * 5,
        scratch_shapes=[
            pltpu.VMEM((CAP_OWN, 128, 128), jnp.bfloat16),
            pltpu.VMEM((CAP_OWN,), jnp.bfloat16),
            own, own, own,
            dma((CAP_OWN // GROUP + 4,)),
            dma((CAP_OWN // GROUP + 4,)),
        ],
        compiler_params=pltpu.CompilerParams(vmem_limit_bytes=VMEM_LIMIT),
        name="finish",
    )(*found)
    shape = (tiles, rows, lanes)
    return master_new.reshape(shape), first_new.reshape(shape), second_new.reshape(shape), codes, rollout_scales


def solution(mesh):
    split = P("fsdp", "replica", None)
    return jax.shard_map(
        on_device,
        mesh=mesh,
        in_specs=(split, split, split, split, P()),
        out_specs=(split, split, split, P("fsdp", None, None), P("fsdp")),
        check_vma=False,
    )
```
